32 devices in a mesh: band: 8 (over z, y), grid: 4 (over x, core).
Axes of the slice: x: 2, y: 2, z: 4, core: 2. Of those that a mesh axis runs over, the one named last changes fastest.
Arguments:
- orbitals: bfloat16 [512, 64, 4096], P('band', 'grid'), may hold values from -6 to 6
- picks: int32 [1], replicated, may hold values from 0 to 511
Outputs:
- exchange_vectors: bfloat16 [512, 64, 4096], P('band', 'grid')
- gram: float32 [512, 512], P('band')
The draws below stay inside these ranges and needn't reach their ends.
All inputs are finite; a program needn't handle non-finite values.
Results may differ from the reference program's by a relative error of at most 0.00085.
Values may be sent and summed in bfloat16 or wider, within the bound.
A program may use at most 192 MiB of HBM per device.

```python
import jax
import jax.numpy as jnp
from jax import lax

NB = 512
NG = 64
NPICK = 1
NPTS = 262144


def levels(rng, extent, split, low, top_value):
    def one(axis_at, parts):
        draws = jax.random.uniform(jax.random.fold_in(jax.random.fold_in(rng, 6), axis_at), (parts,), jnp.float32, low / len(split), top_value / len(split))
        return jnp.repeat(jnp.exp(draws), extent[axis_at] // parts).reshape((-1,) + (1,) * (len(extent) - axis_at - 1))

    factor_of = one(*split[0])
    for cut in split[1:]:
        factor_of = factor_of * one(*cut)
    return factor_of


def centred(own_key, shape, deviation, bound, cuts=(), kind=jnp.bfloat16):
    array = jax.random.normal(own_key, shape, jnp.float32) * deviation
    if len(cuts) > 0:
        array = levels(own_key, shape, cuts, -0.22, 0.18) * array
    return jnp.clip(array, min=-bound, max=bound).astype(kind)


def setup_inputs(seed: int = 0) -> dict:
    key_of = jax.random.split(jax.random.key(seed), 3)
    return {
        "orbitals": centred(key_of[0], (NB, NG, NG * NG), 1.0, 6.0, ((0, 8), (1, 4))),
        "picks": jax.random.randint(key_of[1], (NPICK,), 0, NB).astype(jnp.int32),
    }


KERNEL_SCALE = 128.0


def kernel_table():
    frequency = jnp.arange(NG, dtype=jnp.int32)
    folded = jnp.minimum(frequency, NG - frequency).astype(jnp.float32)
    square = folded * folded
    summed = square[:, None, None] + square[None, :, None] + square[None, None, :]
    return jnp.where(summed > 0, KERNEL_SCALE / jnp.maximum(summed, 1.0), 0.0)


def reference(orbitals, picks):
    cubes = orbitals.reshape(NB, NG, NG, NG)
    chosen = jnp.take(cubes, picks, axis=0).astype(jnp.float32)
    table = kernel_table()

    def block_vectors(rows):
        values = rows.astype(jnp.float32)
        accumulated = jnp.zeros(values.shape, jnp.float32)
        for position in range(NPICK):
            partner = chosen[position]
            density = values * partner[None]
            spectrum = jnp.fft.fftn(density, axes=(1, 2, 3))
            potential = jnp.real(jnp.fft.ifftn(spectrum * table[None], axes=(1, 2, 3)))
            accumulated = accumulated - potential * partner[None]
        return accumulated.astype(jnp.bfloat16)

    block_rows = min(NB, 64)
    vectors = lax.map(block_vectors, cubes.reshape(NB // block_rows, block_rows, NG, NG, NG))
    vectors = vectors.reshape(NB, NG, NG * NG)
    flat_orbitals = orbitals.reshape(NB, NPTS)
    flat_vectors = vectors.reshape(NB, NPTS)
    gram = lax.dot_general(flat_orbitals, flat_vectors, (((1,), (1,)), ((), ())), preferred_element_type=jnp.float32) / NPTS
    return vectors, gram
```

```python
import math
import jax, jax.numpy as jnp
from jax import lax
from jax.experimental import pallas as pl
from jax.experimental.pallas import tpu as pltpu
from jax.sharding import PartitionSpec as P

NG = 64
NPTS = NG ** 3
KERNEL_SCALE = 128.0
LANES = 128
BF = jnp.bfloat16
F32 = jnp.float32
HALF = NG // 2
XW = 512
PLANES = 32
TILE = 16
SWAP = 256


def cas_matrix(length):
    products = (
        jnp.arange(length, dtype=jnp.int32)[:, None]
        * jnp.arange(length, dtype=jnp.int32)[None, :]
        % length
    )
    angles = products.astype(F32) * (2.0 * math.pi / length)
    return jnp.cos(angles) + jnp.sin(angles)


def halves(value):
    high = value.astype(BF)
    return high, (value - high.astype(F32)).astype(BF)


def matrix_halves(value):
    high = lax.reduce_precision(value, 8, 7)
    return high.astype(BF), (value - high).astype(BF)


def kernel_table():
    frequency = jnp.arange(NG, dtype=jnp.int32)
    folded = jnp.minimum(frequency, NG - frequency).astype(F32)
    square = folded * folded
    summed = square[:, None, None] + square[None, :, None] + square[None, None, :]
    table = jnp.where(summed > 0, KERNEL_SCALE / NPTS / jnp.maximum(summed, 1.0), 0.0)
    return table.reshape(NG // 4, 4, NG, NG).transpose(0, 2, 1, 3).reshape(NG // 4, NG, 4 * NG)


def row_factor(matrix):
    high, low = matrix_halves(matrix)
    return jnp.concatenate([high, high, low], axis=1)


def lane_factor(matrix):
    high, low = matrix_halves(jnp.kron(jnp.eye(2, dtype=F32), matrix))
    upper = jnp.concatenate([high, low], axis=1)
    lower = jnp.concatenate([high, jnp.zeros_like(low)], axis=1)
    return jnp.concatenate([upper, lower], axis=0)


def dot(a, b):
    return jnp.dot(a, b, preferred_element_type=F32)


def solve_body(groups, *refs):
    ins, refs = refs[:groups], refs[groups:]
    partner, table, x_there, x_back, y_there, y_back, z_both = refs[:7]
    outs, work = refs[7:7 + groups], refs[7 + groups]
    rows = NG // groups

    def along_rows(factor, value):
        high, low = halves(value)
        return dot(factor[...], jnp.concatenate([high, low, high], axis=0))

    def along_lanes(value):
        high, low = halves(value)
        both = dot(jnp.concatenate([high, low], axis=1), z_both[...])
        return both[:, :LANES] + both[:, LANES:]

    @pl.loop(0, NG * NG // XW, unroll=4)
    def _(i):
        at = pl.ds(pl.multiple_of(i * XW, XW), XW)
        field = jnp.concatenate([ref[0, :, at].astype(F32) for ref in ins], axis=0)
        field = along_rows(x_there, field * partner[:, at].astype(F32))
        for tile in range(XW // LANES):
            work[pl.ds(i * (XW // LANES) + tile, NG, stride=HALF), :] = field[:, tile * LANES:(tile + 1) * LANES]

    @pl.loop(0, NG // PLANES, unroll=2)
    def _(i):
        left = lax.broadcasted_iota(jnp.int32, (HALF, LANES), 1) < NG
        base = i * PLANES * HALF
        parts = []
        for pair in range(PLANES // 2):
            a = work[pl.ds(base + pair * NG, HALF), :]
            b = work[pl.ds(base + pair * NG + HALF, HALF), :]
            parts.append(jnp.where(left, a, pltpu.roll(b, NG, 1)))
            parts.append(jnp.where(left, pltpu.roll(a, NG, 1), b))
        field = along_lanes(jnp.concatenate(parts, axis=0))
        done = []
        for quad in range(PLANES // 4):
            wide = jnp.concatenate(
                [field[quad * 128:quad * 128 + 64], field[quad * 128 + 64:quad * 128 + 128]], axis=1
            )
            wide = along_rows(y_there, wide) * table[i * (PLANES // 4) + quad]
            wide = along_rows(y_back, wide)
            done.append(wide[:, :LANES])
            done.append(wide[:, LANES:])
        field = along_lanes(jnp.concatenate(done, axis=0))
        for pair in range(PLANES // 2):
            u = field[pair * NG:pair * NG + HALF]
            v = field[pair * NG + HALF:pair * NG + NG]
            work[pl.ds(base + pair * NG, HALF), :] = jnp.where(left, u, pltpu.roll(v, NG, 1))
            work[pl.ds(base + pair * NG + HALF, HALF), :] = jnp.where(left, pltpu.roll(u, NG, 1), v)

    @pl.loop(0, NG * NG // XW, unroll=4)
    def _(i):
        at = pl.ds(pl.multiple_of(i * XW, XW), XW)
        field = jnp.concatenate(
            [work[pl.ds(i * (XW // LANES) + tile, NG, stride=HALF), :] for tile in range(XW // LANES)], axis=1
        )
        field = (-along_rows(x_back, field) * partner[:, at].astype(F32)).astype(BF)
        for index, ref in enumerate(outs):
            ref[0, :, at] = field[index * rows:(index + 1) * rows]


def factors(planes_at):
    matrix = cas_matrix(NG)
    by_plane = jnp.take(matrix, planes_at, axis=1)
    by_line = matrix.reshape(NG, HALF, 2).transpose(0, 2, 1).reshape(NG, NG)
    return (
        kernel_table(), row_factor(by_plane), row_factor(by_plane.T),
        row_factor(by_line), row_factor(by_line.T), lane_factor(matrix),
    )


def solve(pieces, partner, fixed):
    groups = len(pieces)
    count, rows, square = pieces[0].shape
    block = pl.BlockSpec((1, rows, square), lambda i: (i, 0, 0))
    whole = lambda array: pl.BlockSpec(array.shape, lambda i: (0,) * array.ndim)
    fixed = (partner,) + fixed
    return pl.pallas_call(
        lambda *refs: solve_body(groups, *refs),
        grid=(count,),
        in_specs=[block] * groups + [whole(a) for a in fixed],
        out_specs=[block] * groups,
        out_shape=[jax.ShapeDtypeStruct(p.shape, BF) for p in pieces],
        scratch_shapes=[pltpu.VMEM((NG * HALF, LANES), F32)],
        compiler_params=pltpu.CompilerParams(vmem_limit_bytes=32 * 1024 * 1024),
        cost_estimate=pl.CostEstimate(
            flops=count * 12 * NG * NG * NG * 256, bytes_accessed=4 * count * NPTS, transcendentals=0
        ),
    )(*pieces, *fixed)


def order_body(pieces, rows, *refs):
    sources, refs = refs[:pieces], refs[pieces:]
    keep_a, keep_b, send_a, send_b, natural, held, sem, out_sem = refs
    me = lax.axis_index("grid")
    share = held.shape[0] // pieces
    copies = []
    for index, source in enumerate(sources):
        place = pl.multiple_of((me ^ index) * share, share)
        copies.append(pltpu.make_async_copy(source, held.at[pl.ds(place, share)], sem.at[index]))
    for copy in copies:
        copy.start()
    for copy in copies:
        copy.wait()
    out = pltpu.make_async_copy(held, natural, out_sem)
    out.start()
    swap_into(held, (keep_a, keep_b), (send_a, send_b))
    out.wait()


def swap_into(held, keep, send):
    width = held.shape[2] // 2
    mine = lax.axis_index("band") % 2

    @pl.loop(0, width // SWAP)
    def _(i):
        for at, outs in ((mine, keep), (1 - mine, send)):
            lanes = pl.ds(pl.multiple_of(at * width + i * SWAP, SWAP), SWAP)
            turned = jnp.swapaxes(held[:, :, lanes], 0, 1)
            half = turned.shape[0] // 2
            put = pl.ds(pl.multiple_of(i * SWAP, SWAP), SWAP)
            outs[0][:, :, put] = turned[:half]
            outs[1][:, :, put] = turned[half:]


def order_vectors(pieces):
    count, rows, square = pieces[0].shape
    bands = count * len(pieces)
    part = jax.ShapeDtypeStruct((rows // 2, bands, square // 2), BF)
    return pl.pallas_call(
        lambda *refs: order_body(len(pieces), rows, *refs),
        in_specs=[pl.BlockSpec(memory_space=pl.ANY)] * len(pieces),
        out_specs=[pl.BlockSpec(memory_space=pltpu.VMEM)] * 4 + [pl.BlockSpec(memory_space=pl.ANY)],
        out_shape=[part] * 4 + [jax.ShapeDtypeStruct((bands, rows, square), BF)],
        scratch_shapes=[
            pltpu.VMEM((bands, rows, square), BF),
            pltpu.SemaphoreType.DMA((len(pieces),)),
            pltpu.SemaphoreType.DMA,
        ],
        compiler_params=pltpu.CompilerParams(vmem_limit_bytes=24 * 1024 * 1024),
        cost_estimate=pl.CostEstimate(flops=0, bytes_accessed=6 * bands * rows * square, transcendentals=0),
    )(*pieces)


def order_orbitals(orbitals):
    bands, rows, square = orbitals.shape
    part = jax.ShapeDtypeStruct((rows // 2, bands, square // 2), BF)
    spec = pl.BlockSpec((rows // 2, TILE, square // 2), lambda i: (0, i, 0))
    return pl.pallas_call(
        lambda held, a, b, c, d: swap_into(held, (a, b), (c, d)),
        grid=(bands // TILE,),
        in_specs=[pl.BlockSpec((TILE, rows, square), lambda i: (i, 0, 0))],
        out_specs=[spec] * 4,
        out_shape=[part] * 4,
        compiler_params=pltpu.CompilerParams(vmem_limit_bytes=24 * 1024 * 1024),
        cost_estimate=pl.CostEstimate(flops=0, bytes_accessed=4 * orbitals.size, transcendentals=0),
    )(orbitals)


def blocks_body(sizes, *refs):
    out = refs[-1]
    values, at = [], 0
    for size in sizes:
        values.append(jnp.concatenate([ref[0] for ref in refs[at:at + size]], axis=0))
        at += size
    o1, o2, x1, x2, x3, x4, e1, e2, y1, y2, y3, y4 = values

    def across(a, b):
        return lax.dot_general(a, b, (((1,), (1,)), ((), ())), preferred_element_type=F32)

    @pl.when(pl.program_id(0) == 0)
    def _():
        out[...] = jnp.zeros_like(out)

    size = out.shape[1]
    first = across(jnp.concatenate([o1, x1, x2, x3], axis=0), e1)
    second = across(jnp.concatenate([o2, x4], axis=0), e2)
    third = across(o2, jnp.concatenate([y1, y2, y3], axis=0))
    out[0] += first[:size] + second[:size]
    out[1] += first[size:2 * size] + second[size:]
    out[2] += first[2 * size:3 * size]
    out[3] += first[3 * size:]
    out[4] += third[:, :size] + across(o1, y4)
    out[5] += third[:, size:2 * size]
    out[6] += third[:, 2 * size:]


def blocks(families):
    sizes = [len(family) for family in families]
    arrays = [array for family in families for array in family]
    planes = arrays[0].shape[0]
    size = sum(array.shape[1] for array in families[0])
    points = arrays[0].shape[2]
    return pl.pallas_call(
        lambda *refs: blocks_body(sizes, *refs),
        grid=(planes,),
        in_specs=[pl.BlockSpec((1,) + a.shape[1:], lambda i: (i, 0, 0)) for a in arrays],
        out_specs=pl.BlockSpec((7, size, size), lambda i: (0, 0, 0)),
        out_shape=jax.ShapeDtypeStruct((7, size, size), F32),
        compiler_params=pltpu.CompilerParams(vmem_limit_bytes=40 * 1024 * 1024),
        cost_estimate=pl.CostEstimate(
            flops=20 * size * size * planes * points,
            bytes_accessed=2 * sum(a.size for a in arrays), transcendentals=0,
        ),
    )(*arrays)


def shift(values, step, layers):
    pairs = [(2 * z + y, 2 * (z + step) + y) for z in layers for y in range(2)]
    return [lax.ppermute(v, "band", pairs) for v in values]


def flip(value, axis, bits):
    return lax.ppermute(value, axis, [(i, i ^ bits) for i in range(lax.axis_size(axis))])


def summed_rows(parts):
    rank = lax.axis_index("band")
    layer, line = rank // 2, rank % 2
    half = parts.shape[1] // 2

    def plain(block):
        own_rows = jnp.where(line == 0, block, jnp.roll(block, half, 0))
        return jnp.where(line == 0, own_rows, jnp.roll(own_rows, half, 1))

    rows = []
    for other in range(lax.axis_size("band") // 2):
        total = jnp.where(layer == other, parts[0], 0.0)
        for step in range(1, 4):
            if other - step >= 0:
                total = jnp.where(layer == other - step, parts[3 + step], total)
            if other + step < 4:
                total = jnp.where(layer == other + step, parts[step].T, total)
        rows.append(plain(total))
    rows = jnp.stack(rows) * (1.0 / NPTS)
    size = rows.shape[1]
    keep = lax.dynamic_slice_in_dim(rows, line * half, half, 1)
    give = lax.dynamic_slice_in_dim(rows, (1 - line) * half, half, 1)
    total = keep + flip(give, "band", 1)
    bit = 1
    while bit < lax.axis_size("grid"):
        total = total + flip(total, "grid", bit)
        bit *= 2
    return total


def reduce_blocks(parts):
    rank = lax.axis_index("band")
    layer = rank // 2
    layers = lax.axis_size("band") // 2
    rows = summed_rows(parts)
    half, size = rows.shape[1:]
    result = rows
    for bits in range(1, layers):
        there = layer ^ bits
        block = lax.dynamic_index_in_dim(rows, there, 0, keepdims=False)
        both = [flip(block, "band", 2 * bits), flip(block, "band", 2 * bits + 1)]
        line = rank % 2
        low = jnp.where(line == 0, both[0], both[1])
        high = jnp.where(line == 0, both[1], both[0])
        whole = jnp.concatenate([low, high], axis=0)
        mine = lax.dynamic_slice_in_dim(whole, line * half, half, 1).T
        result = lax.dynamic_update_index_in_dim(result, block + mine, there, 0)
    return result.transpose(1, 0, 2).reshape(half, layers * size)


def gram_body(left, right, out):
    @pl.when(pl.program_id(0) == 0)
    def _():
        out[...] = jnp.zeros_like(out)

    size = out.shape[0]
    a = left[:, 0].reshape(size, left.shape[3])
    b = right[:, 0].reshape(size, right.shape[3])
    out[...] += lax.dot_general(a, b, (((1,), (1,)), ((), ())), preferred_element_type=F32)


def gram_product(left, right):
    shares, planes, bands, points = left.shape
    size = shares * bands
    if bands % 16 or points % 128:
        return jnp.einsum("gxbk,hxck->gbhc", left, right, preferred_element_type=F32).reshape(size, size)
    block = pl.BlockSpec((shares, 1, bands, points), lambda i: (0, i, 0, 0))
    return pl.pallas_call(
        gram_body,
        grid=(planes,),
        in_specs=[block, block],
        out_specs=pl.BlockSpec((size, size), lambda i: (0, 0)),
        out_shape=jax.ShapeDtypeStruct((size, size), F32),
        compiler_params=pltpu.CompilerParams(vmem_limit_bytes=32 * 1024 * 1024),
        cost_estimate=pl.CostEstimate(
            flops=2 * size * size * planes * points, bytes_accessed=4 * left.size, transcendentals=0
        ),
    )(left, right)


def to_shares(array):
    shares = lax.axis_size("band")
    bands, planes, square = array.shape
    cut = array.reshape(bands, planes, shares, square // shares).transpose(2, 1, 0, 3)
    return lax.all_to_all(cut, "band", split_axis=0, concat_axis=0)


def spread(orbitals, target):
    bands = orbitals.shape[0]
    mine = lax.dynamic_index_in_dim(orbitals, target % bands, 0, keepdims=False)
    slab = jnp.where(lax.axis_index("band") == target // bands, mine, 0).astype(BF)
    bit = 1
    while bit < lax.axis_size("band"):
        slab = slab + flip(slab, "band", bit)
        bit *= 2
    groups = lax.axis_size("grid")
    return jnp.concatenate([slab] + [flip(slab, "grid", d) for d in range(1, groups)], axis=0)


def per_device(orbitals, picks):
    bands, planes, square = orbitals.shape
    groups, shares = lax.axis_size("grid"), lax.axis_size("band")
    me = lax.axis_index("grid")
    tiled = shares == 8 and bands % TILE == 0 and planes % 16 == 0
    chunk = TILE if bands % TILE == 0 else bands
    count = chunk // groups
    order = (me ^ jnp.arange(groups, dtype=jnp.int32))[:, None] * planes
    fixed = factors((order + jnp.arange(planes, dtype=jnp.int32)[None]).reshape(-1))
    partner = spread(orbitals, picks[0])

    if tiled:
        keep1, keep2, send1, send2 = order_orbitals(orbitals)
        o1 = [keep1, flip(send1, "band", 1)]
        o2 = [keep2, flip(send2, "band", 1)]
        x1 = shift(o1, 1, (0, 1))
        x2 = shift(x1, 1, (1, 2))
        x3 = shift(x2, 1, (2,))
        x4 = shift(o2, 1, (0,))

    vectors, e1, e2 = [], [[], []], [[], []]
    y1, y2, y3, y4 = [[], []], [[], []], [[], []], [[], []]
    for start in range(0, bands, chunk):
        pieces = []
        for d in range(groups):
            part = lax.dynamic_slice_in_dim(orbitals, start + (me ^ d) * count, count, 0)
            pieces.append(flip(part, "grid", d) if d else part)
        solved = solve(pieces, partner, fixed)
        back = [flip(p, "grid", d) if d else p for d, p in enumerate(solved)]
        if tiled:
            keep1, keep2, send1, send2, natural = order_vectors(back)
            vectors.append(natural)
            now1 = [keep1, flip(send1, "band", 1)]
            now2 = [keep2, flip(send2, "band", 1)]
            step1 = shift(now2, -1, (3, 2))
            step2 = shift(step1, -1, (2, 1))
            step3 = shift(step2, -1, (1,))
            step4 = shift(now1, -1, (3,))
            for into, values in ((e1, now1), (e2, now2), (y1, step1), (y2, step2), (y3, step3), (y4, step4)):
                into[0].append(values[0])
                into[1].append(values[1])
        else:
            stacked = jnp.take(jnp.stack(back), me ^ jnp.arange(groups), axis=0)
            vectors.append(stacked.reshape(chunk, planes, square))
    vectors = vectors[0] if len(vectors) == 1 else jnp.concatenate(vectors, axis=0)
    if tiled:
        families = [o1, o2, x1, x2, x3, x4] + [f[0] + f[1] for f in (e1, e2, y1, y2, y3, y4)]
        gram = reduce_blocks(blocks(families))
    else:
        product = gram_product(to_shares(orbitals), to_shares(vectors))
        rows = lax.psum_scatter(product * (1.0 / NPTS), "band", scatter_dimension=0, tiled=True)
        gram = lax.psum(rows, "grid")
    return (vectors, gram)


def solution(mesh):
    return jax.shard_map(
        per_device,
        mesh=mesh,
        in_specs=(P("band", "grid", None), P()),
        out_specs=(P("band", "grid", None), P("band", None)),
        check_vma=False,
    )
```

```python
import math
import jax, jax.numpy as jnp
from jax import lax
from jax.experimental import pallas as pl
from jax.experimental.pallas import tpu as pltpu
from jax.sharding import PartitionSpec as P

NG = 64
NPTS = NG ** 3
KERNEL_SCALE = 128.0
LANES = 128
BF = jnp.bfloat16
F32 = jnp.float32
HALF = NG // 2
XW = 512
PLANES = 32
TILE = 16
SWAP = 256
HELD = ({2: (3,), 3: (4,)}, {0: (1, 2), 2: (3,), 3: (4,)}, {1: (1,), 0: (2,), 3: (3, 4)}, {1: (1,), 0: (2,)})


def cas_matrix(length):
    products = (
        jnp.arange(length, dtype=jnp.int32)[:, None]
        * jnp.arange(length, dtype=jnp.int32)[None, :]
        % length
    )
    angles = products.astype(F32) * (2.0 * math.pi / length)
    return jnp.cos(angles) + jnp.sin(angles)


def halves(value):
    high = value.astype(BF)
    return high, (value - high.astype(F32)).astype(BF)


def matrix_halves(value):
    high = lax.reduce_precision(value, 8, 7)
    return high.astype(BF), (value - high).astype(BF)


def kernel_table():
    frequency = jnp.arange(NG, dtype=jnp.int32)
    folded = jnp.minimum(frequency, NG - frequency).astype(F32)
    square = folded * folded
    summed = square[:, None, None] + square[None, :, None] + square[None, None, :]
    table = jnp.where(summed > 0, KERNEL_SCALE / NPTS / jnp.maximum(summed, 1.0), 0.0)
    return table.reshape(NG // 4, 4, NG, NG).transpose(0, 2, 1, 3).reshape(NG // 4, NG, 4 * NG)


def row_factor(matrix):
    high, low = matrix_halves(matrix)
    return jnp.concatenate([high, high, low], axis=1)


def lane_factor(matrix):
    high, low = matrix_halves(jnp.kron(jnp.eye(2, dtype=F32), matrix))
    upper = jnp.concatenate([high, low], axis=1)
    lower = jnp.concatenate([high, jnp.zeros_like(low)], axis=1)
    return jnp.concatenate([upper, lower], axis=0)


def dot(a, b):
    return jnp.dot(a, b, preferred_element_type=F32)


def solve_one(ins, partner, table, x_there, x_back, y_there, y_back, z_both, outs, work):
    rows = NG // len(ins)

    def along_rows(factor, value):
        high, low = halves(value)
        return dot(factor[...], jnp.concatenate([high, low, high], axis=0))

    def along_lanes(value):
        high, low = halves(value)
        both = dot(jnp.concatenate([high, low], axis=1), z_both[...])
        return both[:, :LANES] + both[:, LANES:]

    @pl.loop(0, NG * NG // XW, unroll=4)
    def _(i):
        at = pl.ds(pl.multiple_of(i * XW, XW), XW)
        field = jnp.concatenate([ref[:, at].astype(F32) for ref in ins], axis=0)
        field = along_rows(x_there, field * partner[:, at].astype(F32))
        for tile in range(XW // LANES):
            work[pl.ds(i * (XW // LANES) + tile, NG, stride=HALF), :] = field[:, tile * LANES:(tile + 1) * LANES]

    @pl.loop(0, NG // PLANES, unroll=2)
    def _(i):
        left = lax.broadcasted_iota(jnp.int32, (HALF, LANES), 1) < NG
        base = i * PLANES * HALF
        parts = []
        for pair in range(PLANES // 2):
            a = work[pl.ds(base + pair * NG, HALF), :]
            b = work[pl.ds(base + pair * NG + HALF, HALF), :]
            parts.append(jnp.where(left, a, pltpu.roll(b, NG, 1)))
            parts.append(jnp.where(left, pltpu.roll(a, NG, 1), b))
        field = along_lanes(jnp.concatenate(parts, axis=0))
        done = []
        for quad in range(PLANES // 4):
            wide = jnp.concatenate(
                [field[quad * 128:quad * 128 + 64], field[quad * 128 + 64:quad * 128 + 128]], axis=1
            )
            wide = along_rows(y_there, wide) * table[i * (PLANES // 4) + quad]
            wide = along_rows(y_back, wide)
            done.append(wide[:, :LANES])
            done.append(wide[:, LANES:])
        field = along_lanes(jnp.concatenate(done, axis=0))
        for pair in range(PLANES // 2):
            u = field[pair * NG:pair * NG + HALF]
            v = field[pair * NG + HALF:pair * NG + NG]
            work[pl.ds(base + pair * NG, HALF), :] = jnp.where(left, u, pltpu.roll(v, NG, 1))
            work[pl.ds(base + pair * NG + HALF, HALF), :] = jnp.where(left, pltpu.roll(u, NG, 1), v)

    @pl.loop(0, NG * NG // XW, unroll=4)
    def _(i):
        at = pl.ds(pl.multiple_of(i * XW, XW), XW)
        field = jnp.concatenate(
            [work[pl.ds(i * (XW // LANES) + tile, NG, stride=HALF), :] for tile in range(XW // LANES)], axis=1
        )
        field = (-along_rows(x_back, field) * partner[:, at].astype(F32)).astype(BF)
        for index, ref in enumerate(outs):
            ref[:, at] = field[index * rows:(index + 1) * rows]


def solve_body(groups, *refs):
    ins, outs = refs[:groups], refs[groups + 7:2 * groups + 7]
    solve_one([ref.at[0] for ref in ins], *refs[groups:groups + 7], [ref.at[0] for ref in outs], refs[-1])


def factors(planes_at):
    matrix = cas_matrix(NG)
    by_plane = jnp.take(matrix, planes_at, axis=1)
    by_line = matrix.reshape(NG, HALF, 2).transpose(0, 2, 1).reshape(NG, NG)
    return (
        kernel_table(), row_factor(by_plane), row_factor(by_plane.T),
        row_factor(by_line), row_factor(by_line.T), lane_factor(matrix),
    )


def solve(pieces, partner, fixed):
    groups = len(pieces)
    count, rows, square = pieces[0].shape
    block = pl.BlockSpec((1, rows, square), lambda i: (i, 0, 0))
    whole = lambda array: pl.BlockSpec(array.shape, lambda i: (0,) * array.ndim)
    fixed = (partner,) + fixed
    return pl.pallas_call(
        lambda *refs: solve_body(groups, *refs),
        grid=(count,),
        in_specs=[block] * groups + [whole(a) for a in fixed],
        out_specs=[block] * groups,
        out_shape=[jax.ShapeDtypeStruct(p.shape, BF) for p in pieces],
        scratch_shapes=[pltpu.VMEM((NG * HALF, LANES), F32)],
        compiler_params=pltpu.CompilerParams(vmem_limit_bytes=32 * 1024 * 1024),
        cost_estimate=pl.CostEstimate(
            flops=count * 12 * NG * NG * NG * 256, bytes_accessed=4 * count * NPTS, transcendentals=0
        ),
    )(*pieces, *fixed)
def swap_into(held, keep, send):
    width = held.shape[2] // 2
    mine = lax.axis_index("band") % 2

    @pl.loop(0, width // SWAP)
    def _(i):
        put = pl.ds(pl.multiple_of(i * SWAP, SWAP), SWAP)
        for at, out in ((mine, keep), (1 - mine, send)):
            lanes = pl.ds(pl.multiple_of(at * width + i * SWAP, SWAP), SWAP)
            out[:, :, put] = jnp.swapaxes(held[:, :, lanes], 0, 1)


def order_orbitals(orbitals):
    bands, rows, square = orbitals.shape
    part = jax.ShapeDtypeStruct((rows, bands, square // 2), BF)
    spec = pl.BlockSpec((rows, TILE, square // 2), lambda i: (0, i, 0))
    return pl.pallas_call(
        swap_into,
        grid=(bands // TILE,),
        in_specs=[pl.BlockSpec((TILE, rows, square), lambda i: (i, 0, 0))],
        out_specs=[spec] * 2,
        out_shape=[part] * 2,
        compiler_params=pltpu.CompilerParams(vmem_limit_bytes=24 * 1024 * 1024),
        cost_estimate=pl.CostEstimate(flops=0, bytes_accessed=4 * orbitals.size, transcendentals=0),
    )(orbitals)


def whole_body(chunks, groups, *refs):
    (orb, slab, okeep, osend, table, x_there, x_back, y_there, y_back, z_both,
     vectors, opeer, slots, parts,
     cubes, solved, fresh, partner, hyper, ekeep, epeer, esend, lslots, work, obuf, abuf,
     hyper_sem, pick_sem, fwd_sem, own_sem, back_sem, stay_sem, out_sem,
     oy_sem, r_sem, ey_sem, l_sem, load_sem) = refs
    count, rows = cubes.shape[2:4]
    mid = rows // 2
    band, me = lax.axis_index("band"), lax.axis_index("grid")
    layer = band // 2
    peer = band ^ 1
    up, down = lax.rem(band + 2, 8), lax.rem(band + 6, 8)

    def remote(source, target, sems, axis, index):
        return pltpu.make_async_remote_copy(
            src_ref=source, dst_ref=target, send_sem=sems[0], recv_sem=sems[1],
            device_id={axis: index}, device_id_type=pl.DeviceIdType.MESH,
        )

    def sems(array, *at):
        return array.at[(0,) + at], array.at[(1,) + at]

    barrier = pltpu.get_barrier_semaphore()
    for bits in (1, 2, 4, 6):
        pl.semaphore_signal(barrier, inc=1, device_id={"band": band ^ bits}, device_id_type=pl.DeviceIdType.MESH)
    for d in range(1, groups):
        pl.semaphore_signal(barrier, inc=1, device_id={"grid": me ^ d}, device_id_type=pl.DeviceIdType.MESH)
    pl.semaphore_wait(barrier, 3 + groups)

    def forward(c):
        def at(d):
            return orb.at[pl.ds(c * TILE + (me ^ d) * count, count)]
        moves = [remote(at(d), cubes.at[c, d], sems(fwd_sem, c, d - 1), "grid", me ^ d) for d in range(1, groups)]
        return moves, pltpu.make_async_copy(at(0), cubes.at[c, 0], own_sem.at[c])

    def start_forward(c):
        moves, stay = forward(c)
        for move in moves:
            move.start()
        stay.start()

    def back(c, mine):
        def at(d):
            return fresh.at[c, pl.ds((me if mine else me ^ d) * count, count)]
        moves = [remote(solved.at[c % 2, d], at(d), sems(back_sem, c, d - 1), "grid", me ^ d) for d in range(1, groups)]
        return moves, pltpu.make_async_copy(solved.at[c % 2, 0], fresh.at[c, pl.ds(me * count, count)], stay_sem.at[c])

    def r_move(slot, side, source):
        return remote(source, slots.at[slot, side], sems(r_sem, slot, side), "band", up)

    def l_move(slot, side, c, source):
        return remote(source, lslots.at[slot, side, c], sems(l_sem, slot, side, c), "band", down)

    def oy(half):
        at = pl.ds(half * mid, mid)
        return remote(osend.at[at], opeer.at[at], sems(oy_sem, half), "band", peer)

    def ey(c, half):
        at = pl.ds(half * mid, mid)
        return remote(esend.at[c, at], epeer.at[c, at], sems(ey_sem, c, half), "band", peer)

    steps = [remote(slab, hyper.at[0], sems(hyper_sem, 0), "band", band ^ 1)]
    steps.append(remote(hyper.at[3], hyper.at[1], sems(hyper_sem, 1), "band", band ^ 2))
    steps.append(remote(hyper.at[4], hyper.at[2], sems(hyper_sem, 2), "band", band ^ 4))
    mine = pl.ds(0, rows)
    picks = [
        remote(partner.at[mine], partner.at[pl.ds(d * rows, rows)], sems(pick_sem, d - 1), "grid", me ^ d)
        for d in range(1, groups)
    ]
    steps[0].start()
    start_forward(0)
    steps[0].wait_recv()
    hyper[3] = slab[...] + hyper[0]
    steps[1].start()
    steps[1].wait_recv()
    hyper[4] = hyper[3] + hyper[1]
    steps[2].start()
    steps[2].wait_recv()
    partner[mine] = hyper[4] + hyper[2]
    for move in picks:
        move.start()

    def only(layers, moves):
        for at in layers:
            @pl.when(layer == at)
            def _():
                for move in moves:
                    move.start()

    def first_orbitals():
        oy(0).start()
        only((0, 1), [r_move(0, 0, okeep.at[pl.ds(0, mid)])])
        start_forward(1)
        oy(1).start()

    def second_orbitals():
        oy(0).wait_recv()

        @pl.when((layer == 1) | (layer == 2))
        def _():
            r_move(0, 0, slots.at[0, 0]).wait_recv()

        only((1,), [r_move(1, 0, slots.at[0, 0])])
        only((2,), [r_move(0, 0, slots.at[0, 0])])
        only((0, 1), [r_move(0, 1, opeer.at[pl.ds(0, mid)])])

    def third_orbitals():
        @pl.when((layer == 1) | (layer == 2))
        def _():
            r_move(0, 1, slots.at[0, 1]).wait_recv()

        only((1,), [r_move(1, 1, slots.at[0, 1])])

        @pl.when(layer == 2)
        def _():
            r_move(1, 0, slots.at[1, 0]).wait_recv()
            r_move(1, 0, slots.at[1, 0]).start()
            r_move(0, 1, slots.at[0, 1]).start()

        only((0,), [r_move(1, 0, okeep.at[pl.ds(mid, mid)])])

    def fourth_orbitals():
        oy(1).wait_recv()

        @pl.when(layer == 2)
        def _():
            r_move(1, 1, slots.at[1, 1]).wait_recv()
            r_move(1, 1, slots.at[1, 1]).start()

        only((0,), [r_move(1, 1, opeer.at[pl.ds(mid, mid)])])

    def out_move(c):
        return pltpu.make_async_copy(fresh.at[c], vectors.at[pl.ds(c * TILE, TILE)], out_sem.at[c])

    def collect(c):
        moves, stay = back(c, False)
        for move in moves:
            move.wait_recv()
        stay.wait()
        out_move(c).start()
        swap_into(fresh.at[c], ekeep.at[c], esend.at[c])
        ey(c, 1).start()
        ey(c, 0).start()

    def send_vectors(c, side):
        source = epeer if side else ekeep
        low, high = source.at[c, pl.ds(0, mid)], source.at[c, pl.ds(mid, mid)]
        if side:
            ey(c, 1).wait_recv()
        only((2, 3), [l_move(0, side, c, high)])
        if side:
            ey(c, 0).wait_recv()
        only((3,), [l_move(1, side, c, low)])

    def pass_first(c, side):
        @pl.when((layer == 1) | (layer == 2))
        def _():
            l_move(0, side, c, lslots.at[0, side, c]).wait_recv()

        only((2,), [l_move(1, side, c, lslots.at[0, side, c])])
        only((1,), [l_move(0, side, c, lslots.at[0, side, c])])

    def pass_second(c, side):
        @pl.when(layer == 1)
        def _():
            l_move(1, side, c, lslots.at[1, side, c]).wait_recv()
            l_move(1, side, c, lslots.at[1, side, c]).start()

    orbital_steps = (first_orbitals, second_orbitals, third_orbitals, fourth_orbitals)
    orbital_steps[0]()
    for move in picks:
        move.wait_recv()
    for step in range(chunks + 4):
        if step < chunks:
            moves, stay = forward(step)
            for move in moves:
                move.wait_recv()
            stay.wait()
            if step + 2 < chunks:
                start_forward(step + 2)
            if step >= 2:
                moves, _ = back(step - 2, True)
                for move in moves:
                    move.wait_send()

            @pl.loop(0, count)
            def _(j):
                solve_one(
                    [cubes.at[step, d, j] for d in range(groups)], partner, table, x_there, x_back,
                    y_there, y_back, z_both, [solved.at[step % 2, d, j] for d in range(groups)], work,
                )

            moves, stay = back(step, True)
            for move in moves:
                move.start()
            stay.start()
        if 0 <= step - 1 < chunks:
            collect(step - 1)
            send_vectors(step - 1, 0)
        if 0 <= step - 2 < chunks:
            send_vectors(step - 2, 1)
            pass_first(step - 2, 0)
        if 0 < step < 4:
            orbital_steps[step]()
        if 0 <= step - 3 < chunks:
            pass_first(step - 3, 1)
            pass_second(step - 3, 0)
        if 0 <= step - 4 < chunks:
            pass_second(step - 4, 1)

    sides = [(side, c) for side in range(2) for c in range(chunks)]

    @pl.when(layer == 0)
    def _():
        for side, c in sides:
            for slot in range(2):
                l_move(slot, side, c, lslots.at[slot, side, c]).wait_recv()

    @pl.when(layer == 2)
    def _():
        for side, c in sides:
            l_move(1, side, c, lslots.at[1, side, c]).wait_recv()

    @pl.when(layer == 1)
    def _():
        for side in range(2):
            r_move(1, side, slots.at[1, side]).wait_recv()

    @pl.when(layer == 3)
    def _():
        for side in range(2):
            for slot in range(2):
                r_move(slot, side, slots.at[slot, side]).wait_recv()

    def loads(p, at):
        moves = []
        for half in range(2):
            for side, source in enumerate((okeep, opeer)):
                moves.append(pltpu.make_async_copy(
                    source.at[half * mid + p], obuf.at[at, half, side], load_sem.at[at, len(moves)]))
        return moves

    def slot_loads(p, at):
        return [
            pltpu.make_async_copy(slots.at[slot, side, p], abuf.at[at, slot, side], load_sem.at[at, 4 + slot * 2 + side])
            for slot in range(2) for side in range(2)
        ]

    def start_loads(p, at):
        for move in loads(p, at):
            move.start()

        @pl.when(layer > 0)
        def _():
            for move in slot_loads(p, at):
                move.start()

    def across(a, b):
        return lax.dot_general(a, b, (((1,), (1,)), ((), ())), preferred_element_type=F32)

    parts[...] = jnp.zeros_like(parts)
    start_loads(0, 0)

    @pl.loop(0, mid)
    def _(p):
        at = lax.rem(p, 2)

        @pl.when(p + 1 < mid)
        def _():
            start_loads(p + 1, 1 - at)

        for move in loads(p, at):
            move.wait()
        low = jnp.concatenate([obuf[at, 0, side] for side in range(2)], axis=0)
        high = jnp.concatenate([obuf[at, 1, side] for side in range(2)], axis=0)

        def vector_rows(plane):
            return jnp.concatenate([ref[c, plane] for ref in (ekeep, epeer) for c in range(chunks)], axis=0)

        e_low, e_high = vector_rows(p), vector_rows(mid + p)
        parts[0] += across(low, e_low) + across(high, e_high)

        @pl.when(layer > 0)
        def _():
            for move in slot_loads(p, at):
                move.wait()
            first = jnp.concatenate([abuf[at, 0, side] for side in range(2)], axis=0)
            second = jnp.concatenate([abuf[at, 1, side] for side in range(2)], axis=0)
            parts[1] += across(first, e_low)
            parts[2] += across(second, jnp.where(layer == 1, e_high, e_low))

        @pl.when(layer < 3)
        def _():
            first = jnp.concatenate([lslots[0, side, c, p] for side, c in sides], axis=0)
            second = jnp.concatenate([lslots[1, side, c, p] for side, c in sides], axis=0)
            parts[3] += across(high, first)
            parts[4] += across(jnp.where(layer == 2, low, high), second)

    for move in steps + picks:
        move.wait_send()
    for half in range(2):
        oy(half).wait_send()
    for c in range(chunks):
        out_move(c).wait()
        for move in forward(c)[0]:
            move.wait_send()
        for half in range(2):
            ey(c, half).wait_send()
        if c >= chunks - 2:
            for move in back(c, True)[0]:
                move.wait_send()

    @pl.when(layer < 3)
    def _():
        for side in range(2):
            for slot in range(2):
                r_move(slot, side, slots.at[slot, side]).wait_send()

    @pl.when(layer > 0)
    def _():
        for side, c in sides:
            for slot in range(2):
                l_move(slot, side, c, lslots.at[slot, side, c]).wait_send()


def whole(orbitals, slab, okeep, osend, fixed):
    bands, rows, square = orbitals.shape
    groups = lax.axis_size("grid")
    chunks, count = bands // TILE, TILE // groups
    mid, width = rows // 2, square // 2
    anywhere = pl.BlockSpec(memory_space=pl.ANY)
    inside = pl.BlockSpec(memory_space=pltpu.VMEM)
    dma = pltpu.SemaphoreType.DMA
    sides = 2 * bands
    return pl.pallas_call(
        lambda *refs: whole_body(chunks, groups, *refs),
        in_specs=[anywhere, inside, anywhere, anywhere] + [inside] * len(fixed),
        out_specs=[anywhere, anywhere, anywhere, inside],
        out_shape=[
            jax.ShapeDtypeStruct(orbitals.shape, BF),
            jax.ShapeDtypeStruct((rows, bands, width), BF),
            jax.ShapeDtypeStruct((2, 2, mid, bands, width), BF),
            jax.ShapeDtypeStruct((5, sides, sides), F32),
        ],
        scratch_shapes=[
            pltpu.VMEM((chunks, groups, count, rows, square), BF),
            pltpu.VMEM((2, groups, count, rows, square), BF),
            pltpu.VMEM((chunks, TILE, rows, square), BF),
            pltpu.VMEM((NG, square), BF),
            pltpu.VMEM((5, rows, square), BF),
            pltpu.VMEM((chunks, rows, TILE, width), BF),
            pltpu.VMEM((chunks, rows, TILE, width), BF),
            pltpu.VMEM((chunks, rows, TILE, width), BF),
            pltpu.VMEM((2, 2, chunks, mid, TILE, width), BF),
            pltpu.VMEM((NG * HALF, LANES), F32),
            pltpu.VMEM((2, 2, 2, bands, width), BF),
            pltpu.VMEM((2, 2, 2, bands, width), BF),
            dma((2, 3)), dma((2, groups - 1)), dma((2, chunks, groups - 1)), dma((chunks,)),
            dma((2, chunks, groups - 1)), dma((chunks,)), dma((chunks,)),
            dma((2, 2)), dma((2, 2, 2)), dma((2, chunks, 2)), dma((2, 2, 2, chunks)), dma((2, 8)),
        ],
        compiler_params=pltpu.CompilerParams(
            collective_id=0, has_side_effects=True, vmem_limit_bytes=58 * 1024 * 1024
        ),
        cost_estimate=pl.CostEstimate(
            flops=count * chunks * 12 * NG * NG * NG * 256, bytes_accessed=16 * orbitals.size, transcendentals=0
        ),
    )(orbitals, slab, okeep, osend, *fixed)


def flip(value, axis, bits):
    return lax.ppermute(value, axis, [(i, i ^ bits) for i in range(lax.axis_size(axis))])


def summed_rows(parts):
    rank = lax.axis_index("band")
    layer, line = rank // 2, rank % 2
    half = parts.shape[1] // 2

    def plain(block):
        own_rows = jnp.where(line == 0, block, jnp.roll(block, half, 0))
        return jnp.where(line == 0, own_rows, jnp.roll(own_rows, half, 1))

    rows = []
    for other in range(lax.axis_size("band") // 2):
        total = jnp.where(layer == other, parts[0], 0.0)
        for at in range(4):
            blocks = [parts[i] if i > 2 else parts[i].T for i in HELD[at].get(other, ())]
            if blocks:
                total = jnp.where(layer == at, sum(blocks[1:], blocks[0]), total)
        rows.append(plain(total))
    rows = jnp.stack(rows) * (1.0 / NPTS)
    size = rows.shape[1]
    keep = lax.dynamic_slice_in_dim(rows, line * half, half, 1)
    give = lax.dynamic_slice_in_dim(rows, (1 - line) * half, half, 1)
    total = keep + flip(give, "band", 1)
    bit = 1
    while bit < lax.axis_size("grid"):
        total = total + flip(total, "grid", bit)
        bit *= 2
    return total


def reduce_blocks(parts):
    rank = lax.axis_index("band")
    layer = rank // 2
    layers = lax.axis_size("band") // 2
    rows = summed_rows(parts)
    half, size = rows.shape[1:]
    result = rows
    for bits in range(1, layers):
        there = layer ^ bits
        block = lax.dynamic_index_in_dim(rows, there, 0, keepdims=False)
        both = [flip(block, "band", 2 * bits), flip(block, "band", 2 * bits + 1)]
        line = rank % 2
        low = jnp.where(line == 0, both[0], both[1])
        high = jnp.where(line == 0, both[1], both[0])
        whole = jnp.concatenate([low, high], axis=0)
        mine = lax.dynamic_slice_in_dim(whole, line * half, half, 1).T
        result = lax.dynamic_update_index_in_dim(result, block + mine, there, 0)
    return result.transpose(1, 0, 2).reshape(half, layers * size)


def gram_body(left, right, out):
    @pl.when(pl.program_id(0) == 0)
    def _():
        out[...] = jnp.zeros_like(out)

    size = out.shape[0]
    a = left[:, 0].reshape(size, left.shape[3])
    b = right[:, 0].reshape(size, right.shape[3])
    out[...] += lax.dot_general(a, b, (((1,), (1,)), ((), ())), preferred_element_type=F32)


def gram_product(left, right):
    shares, planes, bands, points = left.shape
    size = shares * bands
    if bands % 16 or points % 128:
        return jnp.einsum("gxbk,hxck->gbhc", left, right, preferred_element_type=F32).reshape(size, size)
    block = pl.BlockSpec((shares, 1, bands, points), lambda i: (0, i, 0, 0))
    return pl.pallas_call(
        gram_body,
        grid=(planes,),
        in_specs=[block, block],
        out_specs=pl.BlockSpec((size, size), lambda i: (0, 0)),
        out_shape=jax.ShapeDtypeStruct((size, size), F32),
        compiler_params=pltpu.CompilerParams(vmem_limit_bytes=32 * 1024 * 1024),
        cost_estimate=pl.CostEstimate(
            flops=2 * size * size * planes * points, bytes_accessed=4 * left.size, transcendentals=0
        ),
    )(left, right)


def to_shares(array):
    shares = lax.axis_size("band")
    bands, planes, square = array.shape
    cut = array.reshape(bands, planes, shares, square // shares).transpose(2, 1, 0, 3)
    return lax.all_to_all(cut, "band", split_axis=0, concat_axis=0)


def spread(slab):
    bit = 1
    while bit < lax.axis_size("band"):
        slab = slab + flip(slab, "band", bit)
        bit *= 2
    groups = lax.axis_size("grid")
    return jnp.concatenate([slab] + [flip(slab, "grid", d) for d in range(1, groups)], axis=0)


def per_device(orbitals, picks):
    bands, planes, square = orbitals.shape
    groups, shares = lax.axis_size("grid"), lax.axis_size("band")
    me = lax.axis_index("grid")
    order = (me ^ jnp.arange(groups, dtype=jnp.int32))[:, None] * planes
    fixed = factors((order + jnp.arange(planes, dtype=jnp.int32)[None]).reshape(-1))
    target = picks[0]
    mine = lax.dynamic_index_in_dim(orbitals, target % bands, 0, keepdims=False)
    slab = jnp.where(lax.axis_index("band") == target // bands, mine, 0).astype(BF)

    if shares == 8 and bands == 4 * TILE and planes % 16 == 0:
        vectors, _, _, parts = whole(orbitals, slab, *order_orbitals(orbitals), fixed)
        return (vectors, reduce_blocks(parts))

    partner = spread(slab)
    count = bands // groups
    pieces = []
    for d in range(groups):
        part = lax.dynamic_slice_in_dim(orbitals, (me ^ d) * count, count, 0)
        pieces.append(flip(part, "grid", d) if d else part)
    solved = solve(pieces, partner, fixed)
    back = [flip(p, "grid", d) if d else p for d, p in enumerate(solved)]
    stacked = jnp.take(jnp.stack(back), me ^ jnp.arange(groups), axis=0)
    vectors = stacked.reshape(bands, planes, square)
    product = gram_product(to_shares(orbitals), to_shares(vectors))
    rows = lax.psum_scatter(product * (1.0 / NPTS), "band", scatter_dimension=0, tiled=True)
    return (vectors, lax.psum(rows, "grid"))


def solution(mesh):
    return jax.shard_map(
        per_device,
        mesh=mesh,
        in_specs=(P("band", "grid", None), P()),
        out_specs=(P("band", "grid", None), P("band", None)),
        check_vma=False,
    )
```

```python
import math
import jax, jax.numpy as jnp
from jax import lax
from jax.experimental import pallas as pl
from jax.experimental.pallas import tpu as pltpu
from jax.sharding import PartitionSpec as P

NG = 64
NPTS = NG ** 3
KERNEL_SCALE = 128.0
LANES = 128
BF = jnp.bfloat16
F32 = jnp.float32
HALF = NG // 2
XW = 512
PLANES = 32
TILE = 16
SWAP = 256
LOW = 9
HELD = ({2: (3,), 3: (4,)}, {0: (1, 2), 2: (3,), 3: (4,)}, {1: (1,), 0: (2,), 3: (3, 4)}, {1: (1,), 0: (2,)})


def cas_matrix(length):
    products = (
        jnp.arange(length, dtype=jnp.int32)[:, None]
        * jnp.arange(length, dtype=jnp.int32)[None, :]
        % length
    )
    angles = products.astype(F32) * (2.0 * math.pi / length)
    return jnp.cos(angles) + jnp.sin(angles)


def halves(value):
    high = value.astype(BF)
    return high, (value - high.astype(F32)).astype(BF)


def matrix_halves(value):
    high = lax.reduce_precision(value, 8, 7)
    return high.astype(BF), (value - high).astype(BF)


def kernel_table():
    frequency = jnp.arange(NG, dtype=jnp.int32)
    folded = jnp.minimum(frequency, NG - frequency).astype(F32)
    square = folded * folded
    summed = square[:, None, None] + square[None, :, None] + square[None, None, :]
    table = jnp.where(summed > 0, KERNEL_SCALE / NPTS / jnp.maximum(summed, 1.0), 0.0)
    return table.reshape(NG // 4, 4, NG, NG).transpose(0, 2, 1, 3).reshape(NG // 4, NG, 4 * NG)


def row_factor(matrix):
    high, low = matrix_halves(matrix)
    return jnp.concatenate([high, high, low], axis=1)


def lane_factor(matrix):
    high, low = matrix_halves(jnp.kron(jnp.eye(2, dtype=F32), matrix))
    upper = jnp.concatenate([high, low], axis=1)
    lower = jnp.concatenate([high, jnp.zeros_like(low)], axis=1)
    return jnp.concatenate([upper, lower], axis=0)


def dot(a, b):
    return jnp.dot(a, b, preferred_element_type=F32)


def solve_one(ins, partner, table, x_there, x_back, y_there, y_back, z_both, outs, work):
    rows = NG // len(ins)

    def along_rows(factor, value):
        high, low = halves(value)
        return dot(factor[...], jnp.concatenate([high, low, high], axis=0))

    def along_lanes(value):
        high, low = halves(value)
        both = dot(jnp.concatenate([high, low], axis=1), z_both[...])
        return both[:, :LANES] + both[:, LANES:]

    @pl.loop(0, NG * NG // XW, unroll=4)
    def _(i):
        at = pl.ds(pl.multiple_of(i * XW, XW), XW)
        field = jnp.concatenate([ref[:, at].astype(F32) for ref in ins], axis=0)
        field = along_rows(x_there, field * partner[:, at].astype(F32))
        for tile in range(XW // LANES):
            work[pl.ds(i * (XW // LANES) + tile, NG, stride=HALF), :] = field[:, tile * LANES:(tile + 1) * LANES]

    @pl.loop(0, NG // PLANES, unroll=2)
    def _(i):
        left = lax.broadcasted_iota(jnp.int32, (HALF, LANES), 1) < NG
        base = i * PLANES * HALF
        parts = []
        for pair in range(PLANES // 2):
            a = work[pl.ds(base + pair * NG, HALF), :]
            b = work[pl.ds(base + pair * NG + HALF, HALF), :]
            parts.append(jnp.where(left, a, pltpu.roll(b, NG, 1)))
            parts.append(jnp.where(left, pltpu.roll(a, NG, 1), b))
        field = along_lanes(jnp.concatenate(parts, axis=0))
        done = []
        for quad in range(PLANES // 4):
            wide = jnp.concatenate(
                [field[quad * 128:quad * 128 + 64], field[quad * 128 + 64:quad * 128 + 128]], axis=1
            )
            wide = along_rows(y_there, wide) * table[i * (PLANES // 4) + quad]
            wide = along_rows(y_back, wide)
            done.append(wide[:, :LANES])
            done.append(wide[:, LANES:])
        field = along_lanes(jnp.concatenate(done, axis=0))
        for pair in range(PLANES // 2):
            u = field[pair * NG:pair * NG + HALF]
            v = field[pair * NG + HALF:pair * NG + NG]
            work[pl.ds(base + pair * NG, HALF), :] = jnp.where(left, u, pltpu.roll(v, NG, 1))
            work[pl.ds(base + pair * NG + HALF, HALF), :] = jnp.where(left, pltpu.roll(u, NG, 1), v)

    @pl.loop(0, NG * NG // XW, unroll=4)
    def _(i):
        at = pl.ds(pl.multiple_of(i * XW, XW), XW)
        field = jnp.concatenate(
            [work[pl.ds(i * (XW // LANES) + tile, NG, stride=HALF), :] for tile in range(XW // LANES)], axis=1
        )
        field = (-along_rows(x_back, field) * partner[:, at].astype(F32)).astype(BF)
        for index, ref in enumerate(outs):
            ref[:, at] = field[index * rows:(index + 1) * rows]


def solve_body(groups, *refs):
    ins, outs = refs[:groups], refs[groups + 7:2 * groups + 7]
    solve_one([ref.at[0] for ref in ins], *refs[groups:groups + 7], [ref.at[0] for ref in outs], refs[-1])


def factors(planes_at):
    matrix = cas_matrix(NG)
    by_plane = jnp.take(matrix, planes_at, axis=1)
    by_line = matrix.reshape(NG, HALF, 2).transpose(0, 2, 1).reshape(NG, NG)
    return (
        kernel_table(), row_factor(by_plane), row_factor(by_plane.T),
        row_factor(by_line), row_factor(by_line.T), lane_factor(matrix),
    )


def solve(pieces, partner, fixed):
    groups = len(pieces)
    count, rows, square = pieces[0].shape
    block = pl.BlockSpec((1, rows, square), lambda i: (i, 0, 0))
    whole = lambda array: pl.BlockSpec(array.shape, lambda i: (0,) * array.ndim)
    fixed = (partner,) + fixed
    return pl.pallas_call(
        lambda *refs: solve_body(groups, *refs),
        grid=(count,),
        in_specs=[block] * groups + [whole(a) for a in fixed],
        out_specs=[block] * groups,
        out_shape=[jax.ShapeDtypeStruct(p.shape, BF) for p in pieces],
        scratch_shapes=[pltpu.VMEM((NG * HALF, LANES), F32)],
        compiler_params=pltpu.CompilerParams(vmem_limit_bytes=32 * 1024 * 1024),
        cost_estimate=pl.CostEstimate(
            flops=count * 12 * NG * NG * NG * 256, bytes_accessed=4 * count * NPTS, transcendentals=0
        ),
    )(*pieces, *fixed)
def swap_into(held, keep, send):
    width = held.shape[2] // 2
    mine = lax.axis_index("band") % 2

    @pl.loop(0, width // SWAP)
    def _(i):
        put = pl.ds(pl.multiple_of(i * SWAP, SWAP), SWAP)
        for at, out in ((mine, keep), (1 - mine, send)):
            lanes = pl.ds(pl.multiple_of(at * width + i * SWAP, SWAP), SWAP)
            out[:, :, put] = jnp.swapaxes(held[:, :, lanes], 0, 1)


def order_orbitals(orbitals):
    bands, rows, square = orbitals.shape
    part = jax.ShapeDtypeStruct((rows, bands, square // 2), BF)
    spec = pl.BlockSpec((rows, TILE, square // 2), lambda i: (0, i, 0))
    return pl.pallas_call(
        swap_into,
        grid=(bands // TILE,),
        in_specs=[pl.BlockSpec((TILE, rows, square), lambda i: (i, 0, 0))],
        out_specs=[spec] * 2,
        out_shape=[part] * 2,
        compiler_params=pltpu.CompilerParams(vmem_limit_bytes=24 * 1024 * 1024),
        cost_estimate=pl.CostEstimate(flops=0, bytes_accessed=4 * orbitals.size, transcendentals=0),
    )(orbitals)


def whole_body(chunks, groups, *refs):
    (orb, slab, okeep, osend, table, x_there, x_back, y_there, y_back, z_both,
     vectors, opeer, slots, gram,
     cubes, solved, fresh, partner, hyper, ekeep, epeer, esend, lslots, work, obuf, abuf,
     parts, turned, sums, come, last,
     hyper_sem, pick_sem, fwd_sem, own_sem, back_sem, stay_sem, out_sem,
     oy_sem, r_sem, ey_sem, l_sem, load_sem, sum_sem, last_sem) = refs
    rows = cubes.shape[2]
    bands = cubes.shape[0]
    count = TILE // groups
    ring = solved.shape[0]
    low = lslots.shape[3]
    high = rows - low
    band, me = lax.axis_index("band"), lax.axis_index("grid")
    layer, line = band // 2, band % 2
    peer = band ^ 1
    up, down = lax.rem(band + 2, 8), lax.rem(band + 6, 8)

    def remote(source, target, sems, axis, index):
        return pltpu.make_async_remote_copy(
            src_ref=source, dst_ref=target, send_sem=sems[0], recv_sem=sems[1],
            device_id={axis: index}, device_id_type=pl.DeviceIdType.MESH,
        )

    def sems(array, *at):
        return array.at[(0,) + at], array.at[(1,) + at]

    def start(moves):
        for move in moves:
            move.start()

    def arrive(moves):
        for move in moves:
            move.wait_recv()

    def leave(moves):
        for move in moves:
            move.wait_send()

    def on(*layers):
        hit = layer == layers[0]
        for other in layers[1:]:
            hit = hit | (layer == other)
        return pl.when(hit)

    barrier = pltpu.get_barrier_semaphore()
    for bits in range(1, 8):
        pl.semaphore_signal(barrier, inc=1, device_id={"band": band ^ bits}, device_id_type=pl.DeviceIdType.MESH)
    for d in range(1, groups):
        pl.semaphore_signal(barrier, inc=1, device_id={"grid": me ^ d}, device_id_type=pl.DeviceIdType.MESH)
    pl.semaphore_wait(barrier, 6 + groups)

    def forward(t):
        def at(d):
            return orb.at[(t // count) * TILE + (me ^ d) * count + lax.rem(t, count)]
        moves = [remote(at(d), cubes.at[t, d], sems(fwd_sem, t, d - 1), "grid", me ^ d) for d in range(1, groups)]
        return moves, pltpu.make_async_copy(at(0), cubes.at[t, 0], own_sem.at[t])

    def start_forward(t):
        moves, stay = forward(t)
        start(moves)
        stay.start()

    def back(t, mine):
        def at(d):
            return fresh.at[t // count, (me if mine else me ^ d) * count + lax.rem(t, count)]
        source = lax.rem(t, ring)
        moves = [remote(solved.at[source, d], at(d), sems(back_sem, t, d - 1), "grid", me ^ d) for d in range(1, groups)]
        own = fresh.at[t // count, me * count + lax.rem(t, count)]
        return moves, pltpu.make_async_copy(solved.at[source, 0], own, stay_sem.at[t])

    low_cut = ((0, (low + 1) // 2), ((low + 1) // 2, low // 2))
    high_cut = ((0, (high + 1) // 2), ((high + 1) // 2, high // 2))

    def r_move(slot, side, q, source, first=0, cut=low_cut):
        at, size = cut[q]
        return remote(
            source.at[pl.ds(first + at, size)], slots.at[slot, side, pl.ds(at, size)],
            sems(r_sem, slot, side, q), "band", up,
        )

    def r_pass(slot, side, q, onto):
        return r_move(onto, side, q, slots.at[slot, side])

    def r_here(slot, side, q, cut=low_cut):
        return r_move(slot, side, q, slots.at[slot, side], 0, cut)

    def l_move(slot, side, c, source, first, size):
        return remote(
            source.at[pl.ds(first, size)], lslots.at[slot, side, c, pl.ds(0, size)],
            sems(l_sem, slot, side, c), "band", down,
        )

    def l_here(slot, side, c, size=high):
        return l_move(slot, side, c, lslots.at[slot, side, c], 0, size)

    def oy(half):
        at = pl.ds(low, high) if half else pl.ds(0, low)
        return remote(osend.at[at], opeer.at[at], sems(oy_sem, half), "band", peer)

    def ey(c, half):
        at = pl.ds(low, high) if half else pl.ds(0, low)
        return remote(esend.at[c, at], epeer.at[c, at], sems(ey_sem, c, half), "band", peer)

    steps = [remote(slab, hyper.at[0], sems(hyper_sem, 0), "band", band ^ 1)]
    steps.append(remote(hyper.at[3], hyper.at[1], sems(hyper_sem, 1), "band", band ^ 2))
    steps.append(remote(hyper.at[4], hyper.at[2], sems(hyper_sem, 2), "band", band ^ 4))
    mine = pl.ds(0, rows)
    picks = [
        remote(partner.at[mine], partner.at[pl.ds(d * rows, rows)], sems(pick_sem, d - 1), "grid", me ^ d)
        for d in range(1, groups)
    ]
    steps[0].start()
    start_forward(0)
    start_forward(1)
    steps[0].wait_recv()
    hyper[3] = slab[...] + hyper[0]
    steps[1].start()
    oy(0).start()
    steps[1].wait_recv()
    hyper[4] = hyper[3] + hyper[1]
    steps[2].start()

    @on(0, 1)
    def _():
        start([r_move(0, 0, q, okeep) for q in range(2)])

    steps[2].wait_recv()
    partner[mine] = hyper[4] + hyper[2]
    start(picks)
    start_forward(2)
    start_forward(3)
    oy(1).start()

    def own_orbitals(q):
        @on(1)
        def _():
            r_here(0, 0, q).wait_recv()
            r_pass(0, 0, q, 1).start()

        @on(2)
        def _():
            r_here(0, 0, q).wait_recv()
            r_pass(0, 0, q, 0).start()

        @on(0)
        def _():
            r_move(1, 0, q, okeep, low, high_cut).start()

    def own_orbitals_on(q):
        @on(2)
        def _():
            r_here(1, 0, q).wait_recv()
            r_pass(1, 0, q, 1).start()

        if q == 0:
            oy(0).wait_recv()

            @on(0, 1)
            def _():
                start([r_move(0, 1, part, opeer) for part in range(2)])

    def peer_orbitals(q):
        if q == 0:
            oy(1).wait_recv()

        @on(1)
        def _():
            r_here(0, 1, q).wait_recv()
            r_pass(0, 1, q, 1).start()

        @on(2)
        def _():
            r_here(0, 1, q).wait_recv()
            r_pass(0, 1, q, 0).start()

        @on(0)
        def _():
            r_move(1, 1, q, opeer, low, high_cut).start()

    def peer_orbitals_on(q):
        @on(2)
        def _():
            r_here(1, 1, q).wait_recv()
            r_pass(1, 1, q, 1).start()

    def out_move(c):
        return pltpu.make_async_copy(fresh.at[c], vectors.at[pl.ds(c * TILE, TILE)], out_sem.at[c])

    def collect(c):
        for j in range(count):
            moves, stay = back(c * count + j, False)
            arrive(moves)
            stay.wait()
        out_move(c).start()
        swap_into(fresh.at[c], ekeep.at[c], esend.at[c])
        ey(c, 1).start()
        send_vectors(c, 0)
        ey(c, 0).start()

    def send_vectors(c, side):
        source = (epeer if side else ekeep).at[c]
        if side:
            ey(c, 1).wait_recv()

        @on(2, 3)
        def _():
            l_move(0, side, c, source, low, high).start()

        if side:
            ey(c, 0).wait_recv()

        @on(3)
        def _():
            l_move(1, side, c, source, 0, low).start()

    def pass_first(c, side):
        @on(2)
        def _():
            l_here(0, side, c).wait_recv()
            l_move(1, side, c, lslots.at[0, side, c], 0, high).start()

        @on(1)
        def _():
            l_here(0, side, c).wait_recv()
            l_move(0, side, c, lslots.at[0, side, c], 0, high).start()

    def pass_second(c, side):
        @on(1)
        def _():
            l_here(1, side, c).wait_recv()
            l_move(1, side, c, lslots.at[1, side, c], 0, high).start()

    arrive(picks)
    after = {
        0: [(own_orbitals, 0)],
        3: [(own_orbitals, 1)],
        4: [(own_orbitals_on, 0), (collect, 0)],
        5: [(pass_first, 0, 0)],
        6: [(own_orbitals_on, 1), (send_vectors, 0, 1), (pass_second, 0, 0)],
        7: [(pass_first, 0, 1)],
        8: [(peer_orbitals, 0), (pass_second, 0, 1), (collect, 1)],
        9: [(pass_first, 1, 0)],
        10: [(peer_orbitals, 1), (send_vectors, 1, 1), (pass_second, 1, 0)],
        11: [(pass_first, 1, 1)],
        12: [(peer_orbitals_on, 0), (pass_second, 1, 1), (collect, 2)],
        13: [(pass_first, 2, 0)],
        14: [(peer_orbitals_on, 1), (send_vectors, 2, 1), (pass_second, 2, 0)],
        15: [(pass_first, 2, 1)],
    }

    @pl.loop(0, bands)
    def _(t):
        moves, stay = forward(t)
        arrive(moves)
        stay.wait()

        @pl.when(t >= ring)
        def _():
            leave(back(t - ring, True)[0])

        at = lax.rem(t, ring)
        solve_one(
            [cubes.at[t, d] for d in range(groups)], partner, table, x_there, x_back,
            y_there, y_back, z_both, [solved.at[at, d] for d in range(groups)], work,
        )
        moves, stay = back(t, True)
        start(moves)
        stay.start()

        @pl.when(t + count < bands)
        def _():
            start_forward(t + count)

        for slot, events in after.items():
            @pl.when(t == slot)
            def _():
                for event in events:
                    event[0](*event[1:])

    for event in (
        (pass_second, 2, 1), (collect, 3), (pass_first, 3, 0), (send_vectors, 3, 1),
        (pass_second, 3, 0), (pass_first, 3, 1), (pass_second, 3, 1),
    ):
        event[0](*event[1:])

    sides = [(side, c) for side in range(2) for c in range(chunks)]

    @on(0)
    def _():
        for side, c in sides:
            arrive([l_here(slot, side, c) for slot in range(2)])

    @on(2)
    def _():
        for side, c in sides:
            l_here(1, side, c, low).wait_recv()

    @on(1)
    def _():
        for side in range(2):
            arrive([r_here(1, side, q, high_cut) for q in range(2)])

    @on(3)
    def _():
        for side in range(2):
            for slot in range(2):
                arrive([r_here(slot, side, q) for q in range(2)])

    def loads(p, at):
        return [
            pltpu.make_async_copy(source.at[p], obuf.at[at, side], load_sem.at[at, side])
            for side, source in enumerate((okeep, opeer))
        ]

    def slot_loads(slot, p, at):
        return [
            pltpu.make_async_copy(slots.at[slot, side, p], abuf.at[at, slot, side], load_sem.at[at, 2 + slot * 2 + side])
            for side in range(2)
        ]

    def with_slots(p, at, act):
        @pl.when((layer > 0) & (p < low))
        def _():
            act(0, slot_loads(0, p, at))

        @pl.when((layer > 1) & (p < low))
        def _():
            act(1, slot_loads(1, p, at))

        @pl.when((layer == 1) & (p >= low))
        def _():
            act(1, slot_loads(1, p - low, at))

    def start_loads(p, at):
        start(loads(p, at))
        with_slots(p, at, lambda slot, moves: start(moves))

    def across(a, b):
        return lax.dot_general(a, b, (((1,), (1,)), ((), ())), preferred_element_type=F32)

    parts[...] = jnp.zeros_like(parts)
    start_loads(0, 0)

    @pl.loop(0, rows)
    def _(p):
        at = lax.rem(p, 2)

        @pl.when(p + 1 < rows)
        def _():
            start_loads(p + 1, 1 - at)

        for move in loads(p, at):
            move.wait()
        here = jnp.concatenate([obuf[at, side] for side in range(2)], axis=0)
        there = jnp.concatenate([ref[c, p] for ref in (ekeep, epeer) for c in range(chunks)], axis=0)
        parts[0] += across(here, there)

        def add(slot, moves):
            for move in moves:
                move.wait()
            parts[1 + slot] += across(jnp.concatenate([abuf[at, slot, side] for side in range(2)], axis=0), there)

        with_slots(p, at, add)

        def moved(slot, plane):
            parts[3 + slot] += across(here, jnp.concatenate([lslots[slot, side, c, plane] for side, c in sides], axis=0))

        @pl.when((layer < 3) & (p >= low))
        def _():
            moved(0, p - low)

        @pl.when((layer < 2) & (p >= low))
        def _():
            moved(1, p - low)

        @pl.when((layer == 2) & (p < low))
        def _():
            moved(1, p)

    size = parts.shape[1]
    half = size // 2
    for at in range(chunks):
        @on(at)
        def _():
            for other in range(chunks):
                if other == at:
                    turned[other] = parts[0]
                else:
                    found = [parts[i] if i > 2 else parts[i].T for i in HELD[at].get(other, ())]
                    turned[other] = sum(found[1:], found[0]) if found else jnp.zeros((size, size), F32)
    for other in range(chunks):
        block = turned[other] * (1.0 / NPTS)
        block = jnp.where(line == 1, pltpu.roll(block, half, 1), block)
        sums[0, other] = block[half:]
        sums[1, other] = block[:half]
    totals = [
        remote(sums.at[0], come.at[0], sems(sum_sem, 0), "band", peer),
        remote(sums.at[2], come.at[1], sems(sum_sem, 1), "grid", me ^ 1),
        remote(sums.at[3], come.at[2], sems(sum_sem, 2), "grid", me ^ 2),
    ]
    for i, move in enumerate(totals):
        move.start()
        move.wait_recv()
        sums[2 + i] = sums[1 + i] + come[i]
    swaps = []
    for bits in range(1, chunks):
        block = sums.at[4, layer ^ bits]
        for turn in range(2):
            swaps.append((remote(
                block, last.at[bits - 1, line], sems(last_sem, bits - 1, turn), "band", band ^ (2 * bits + turn)
            ), remote(
                block, last.at[bits - 1, line ^ turn], sems(last_sem, bits - 1, turn), "band", band ^ (2 * bits + turn)
            )))
    for move, _ in swaps:
        move.start()
    gram[:, pl.ds(pl.multiple_of(layer * size, size), size)] = sums[4, layer]
    for _, move in swaps:
        move.wait_recv()
    for bits in range(1, chunks):
        whole_block = jnp.concatenate([last[bits - 1, 0], last[bits - 1, 1]], axis=0).T
        mine_block = jnp.where(line == 0, whole_block[:half], whole_block[half:])
        there = layer ^ bits
        gram[:, pl.ds(pl.multiple_of(there * size, size), size)] = sums[4, there] + mine_block

    leave(steps + picks + totals + [move for move, _ in swaps] + [oy(half) for half in range(2)])

    @pl.loop(0, bands)
    def _(t):
        leave(forward(t)[0])

        @pl.when(t >= bands - ring)
        def _():
            leave(back(t, True)[0])

    for c in range(chunks):
        out_move(c).wait()
        leave([ey(c, half) for half in range(2)])

    @on(0)
    def _():
        for side in range(2):
            leave([r_here(0, side, q) for q in range(2)] + [r_here(1, side, q, high_cut) for q in range(2)])

    @on(1, 2)
    def _():
        for side in range(2):
            leave([r_here(slot, side, q) for slot in range(2) for q in range(2)])

    @on(1, 2, 3)
    def _():
        for side, c in sides:
            l_here(0, side, c).wait_send()

    @on(1, 2)
    def _():
        for side, c in sides:
            l_here(1, side, c).wait_send()

    @on(3)
    def _():
        for side, c in sides:
            l_here(1, side, c, low).wait_send()


def whole(orbitals, slab, okeep, osend, fixed):
    bands, rows, square = orbitals.shape
    groups = lax.axis_size("grid")
    chunks, count = bands // TILE, TILE // groups
    low, width = LOW * rows // 16, square // 2
    ring = min(8, bands // groups)
    anywhere = pl.BlockSpec(memory_space=pl.ANY)
    inside = pl.BlockSpec(memory_space=pltpu.VMEM)
    dma = pltpu.SemaphoreType.DMA
    size = 2 * bands
    solves = bands // groups
    return pl.pallas_call(
        lambda *refs: whole_body(chunks, groups, *refs),
        in_specs=[anywhere, inside, anywhere, anywhere] + [inside] * len(fixed),
        out_specs=[anywhere, anywhere, anywhere, inside],
        out_shape=[
            jax.ShapeDtypeStruct(orbitals.shape, BF),
            jax.ShapeDtypeStruct((rows, bands, width), BF),
            jax.ShapeDtypeStruct((2, 2, low, bands, width), BF),
            jax.ShapeDtypeStruct((bands, 4 * size), F32),
        ],
        scratch_shapes=[
            pltpu.VMEM((solves, groups, rows, square), BF),
            pltpu.VMEM((ring, groups, rows, square), BF),
            pltpu.VMEM((chunks, TILE, rows, square), BF),
            pltpu.VMEM((NG, square), BF),
            pltpu.VMEM((5, rows, square), BF),
            pltpu.VMEM((chunks, rows, TILE, width), BF),
            pltpu.VMEM((chunks, rows, TILE, width), BF),
            pltpu.VMEM((chunks, rows, TILE, width), BF),
            pltpu.VMEM((2, 2, chunks, low, TILE, width), BF),
            pltpu.VMEM((NG * HALF, LANES), F32),
            pltpu.VMEM((2, 2, bands, width), BF),
            pltpu.VMEM((2, 2, 2, bands, width), BF),
            pltpu.VMEM((5, size, size), F32),
            pltpu.VMEM((4, size, size), F32),
            pltpu.VMEM((5, 4, bands, size), F32),
            pltpu.VMEM((3, 4, bands, size), F32),
            pltpu.VMEM((3, 2, bands, size), F32),
            dma((2, 3)), dma((2, groups - 1)), dma((2, solves, groups - 1)), dma((solves,)),
            dma((2, solves, groups - 1)), dma((solves,)), dma((chunks,)),
            dma((2, 2)), dma((2, 2, 2, 2)), dma((2, chunks, 2)), dma((2, 2, 2, chunks)), dma((2, 6)),
            dma((2, 3)), dma((2, 3, 2)),
        ],
        compiler_params=pltpu.CompilerParams(
            collective_id=0, has_side_effects=True, vmem_limit_bytes=60 * 1024 * 1024
        ),
        cost_estimate=pl.CostEstimate(
            flops=solves * 12 * NG * NG * NG * 256, bytes_accessed=16 * orbitals.size, transcendentals=0
        ),
    )(orbitals, slab, okeep, osend, *fixed)


def flip(value, axis, bits):
    return lax.ppermute(value, axis, [(i, i ^ bits) for i in range(lax.axis_size(axis))])


def gram_body(left, right, out):
    @pl.when(pl.program_id(0) == 0)
    def _():
        out[...] = jnp.zeros_like(out)

    size = out.shape[0]
    a = left[:, 0].reshape(size, left.shape[3])
    b = right[:, 0].reshape(size, right.shape[3])
    out[...] += lax.dot_general(a, b, (((1,), (1,)), ((), ())), preferred_element_type=F32)


def gram_product(left, right):
    shares, planes, bands, points = left.shape
    size = shares * bands
    if bands % 16 or points % 128:
        return jnp.einsum("gxbk,hxck->gbhc", left, right, preferred_element_type=F32).reshape(size, size)
    block = pl.BlockSpec((shares, 1, bands, points), lambda i: (0, i, 0, 0))
    return pl.pallas_call(
        gram_body,
        grid=(planes,),
        in_specs=[block, block],
        out_specs=pl.BlockSpec((size, size), lambda i: (0, 0)),
        out_shape=jax.ShapeDtypeStruct((size, size), F32),
        compiler_params=pltpu.CompilerParams(vmem_limit_bytes=32 * 1024 * 1024),
        cost_estimate=pl.CostEstimate(
            flops=2 * size * size * planes * points, bytes_accessed=4 * left.size, transcendentals=0
        ),
    )(left, right)


def to_shares(array):
    shares = lax.axis_size("band")
    bands, planes, square = array.shape
    cut = array.reshape(bands, planes, shares, square // shares).transpose(2, 1, 0, 3)
    return lax.all_to_all(cut, "band", split_axis=0, concat_axis=0)


def spread(slab):
    bit = 1
    while bit < lax.axis_size("band"):
        slab = slab + flip(slab, "band", bit)
        bit *= 2
    groups = lax.axis_size("grid")
    return jnp.concatenate([slab] + [flip(slab, "grid", d) for d in range(1, groups)], axis=0)


def per_device(orbitals, picks):
    bands, planes, square = orbitals.shape
    groups, shares = lax.axis_size("grid"), lax.axis_size("band")
    me = lax.axis_index("grid")
    order = (me ^ jnp.arange(groups, dtype=jnp.int32))[:, None] * planes
    fixed = factors((order + jnp.arange(planes, dtype=jnp.int32)[None]).reshape(-1))
    target = picks[0]
    mine = lax.dynamic_index_in_dim(orbitals, target % bands, 0, keepdims=False)
    slab = jnp.where(lax.axis_index("band") == target // bands, mine, 0).astype(BF)

    if shares == 8 and groups == 4 and bands == 4 * TILE and planes == 16:
        vectors, _, _, gram = whole(orbitals, slab, *order_orbitals(orbitals), fixed)
        return (vectors, gram)

    partner = spread(slab)
    count = bands // groups
    pieces = []
    for d in range(groups):
        part = lax.dynamic_slice_in_dim(orbitals, (me ^ d) * count, count, 0)
        pieces.append(flip(part, "grid", d) if d else part)
    solved = solve(pieces, partner, fixed)
    back = [flip(p, "grid", d) if d else p for d, p in enumerate(solved)]
    stacked = jnp.take(jnp.stack(back), me ^ jnp.arange(groups), axis=0)
    vectors = stacked.reshape(bands, planes, square)
    product = gram_product(to_shares(orbitals), to_shares(vectors))
    rows = lax.psum_scatter(product * (1.0 / NPTS), "band", scatter_dimension=0, tiled=True)
    return (vectors, lax.psum(rows, "grid"))


def solution(mesh):
    return jax.shard_map(
        per_device,
        mesh=mesh,
        in_specs=(P("band", "grid", None), P()),
        out_specs=(P("band", "grid", None), P("band", None)),
        check_vma=False,
    )
```

```python
import math
import jax
import jax.numpy as jnp
import ml_dtypes
import numpy as np
from jax import lax
from jax.experimental import pallas as pl
from jax.experimental.pallas import tpu as pltpu
from jax.sharding import PartitionSpec as P

NG = 64
NPTS = NG ** 3
KERNEL_SCALE = 128.0
LANES = 128
BF = ml_dtypes.bfloat16
F32 = jnp.float32
HALF = NG // 2
XW = 512
PLANES = 32
TILE = 16
SWAP = 256
LOW = 9
MORE = 3
HELD = ({2: (3,), 3: (4,)}, {0: (1, 2), 2: (3,), 3: (4,)}, {1: (1,), 0: (2,), 3: (3, 4)}, {1: (1,), 0: (2,), 2: (5,)})


def cas_matrix(length):
    products = np.arange(length)[:, None] * np.arange(length)[None, :] % length
    angles = products * (2.0 * math.pi / length)
    return (np.cos(angles) + np.sin(angles)).astype(np.float32)


def halves(value):
    high = value.astype(BF)
    return high, (value - high.astype(F32)).astype(BF)


def kernel_table():
    frequency = np.arange(NG)
    folded = np.minimum(frequency, NG - frequency)
    square = folded * folded
    summed = square[:, None, None] + square[None, :, None] + square[None, None, :]
    table = np.where(summed > 0, KERNEL_SCALE / NPTS / np.maximum(summed, 1), 0.0).astype(np.float32)
    return table.reshape(NG // 4, 4, NG, NG).transpose(0, 2, 1, 3).reshape(NG // 4, NG, 4 * NG)


def row_factor(matrix):
    high, low = halves(matrix)
    return np.concatenate([high, high, low], axis=1)


def lane_factor(matrix):
    high, low = halves(np.kron(np.eye(2, dtype=np.float32), matrix))
    upper = np.concatenate([high, low], axis=1)
    lower = np.concatenate([high, np.zeros_like(low)], axis=1)
    return np.concatenate([upper, lower], axis=0)


def dot(a, b):
    return jnp.dot(a, b, preferred_element_type=F32)


def solve_one(ins, partner, table, x_there, x_back, y_there, y_back, z_both, outs, work):
    rows = NG // len(ins)
    me = lax.axis_index("grid")
    x_there, x_back = x_there.at[me], x_back.at[me]

    def along_rows(factor, value):
        high, low = halves(value)
        return dot(factor[...], jnp.concatenate([high, low, high], axis=0))

    def along_lanes(value):
        high, low = halves(value)
        both = dot(jnp.concatenate([high, low], axis=1), z_both[...])
        return both[:, :LANES] + both[:, LANES:]

    @pl.loop(0, NG * NG // XW, unroll=4)
    def _(i):
        at = pl.ds(pl.multiple_of(i * XW, XW), XW)
        field = jnp.concatenate([ref[:, at].astype(F32) for ref in ins], axis=0)
        field = along_rows(x_there, field * partner[:, at].astype(F32))
        for tile in range(XW // LANES):
            work[pl.ds(i * (XW // LANES) + tile, NG, stride=HALF), :] = field[:, tile * LANES:(tile + 1) * LANES]

    @pl.loop(0, NG // PLANES, unroll=2)
    def _(i):
        left = lax.broadcasted_iota(jnp.int32, (HALF, LANES), 1) < NG
        base = i * PLANES * HALF
        parts = []
        for pair in range(PLANES // 2):
            a = work[pl.ds(base + pair * NG, HALF), :]
            b = work[pl.ds(base + pair * NG + HALF, HALF), :]
            parts.append(jnp.where(left, a, pltpu.roll(b, NG, 1)))
            parts.append(jnp.where(left, pltpu.roll(a, NG, 1), b))
        field = along_lanes(jnp.concatenate(parts, axis=0))
        done = []
        for quad in range(PLANES // 4):
            wide = jnp.concatenate(
                [field[quad * 128:quad * 128 + 64], field[quad * 128 + 64:quad * 128 + 128]], axis=1
            )
            wide = along_rows(y_there, wide) * table[i * (PLANES // 4) + quad]
            wide = along_rows(y_back, wide)
            done.append(wide[:, :LANES])
            done.append(wide[:, LANES:])
        field = along_lanes(jnp.concatenate(done, axis=0))
        for pair in range(PLANES // 2):
            u = field[pair * NG:pair * NG + HALF]
            v = field[pair * NG + HALF:pair * NG + NG]
            work[pl.ds(base + pair * NG, HALF), :] = jnp.where(left, u, pltpu.roll(v, NG, 1))
            work[pl.ds(base + pair * NG + HALF, HALF), :] = jnp.where(left, pltpu.roll(u, NG, 1), v)

    @pl.loop(0, NG * NG // XW, unroll=4)
    def _(i):
        at = pl.ds(pl.multiple_of(i * XW, XW), XW)
        field = jnp.concatenate(
            [work[pl.ds(i * (XW // LANES) + tile, NG, stride=HALF), :] for tile in range(XW // LANES)], axis=1
        )
        field = (-along_rows(x_back, field) * partner[:, at].astype(F32)).astype(BF)
        for index, ref in enumerate(outs):
            ref[:, at] = field[index * rows:(index + 1) * rows]


def solve_body(groups, *refs):
    ins, outs = refs[:groups], refs[groups + 7:2 * groups + 7]
    solve_one([ref.at[0] for ref in ins], *refs[groups:groups + 7], [ref.at[0] for ref in outs], refs[-1])


def factors(groups):
    matrix = cas_matrix(NG)
    there, back = [], []
    for me in range(groups):
        order = [slab * (NG // groups) + plane for slab in (me ^ d for d in range(groups)) for plane in range(NG // groups)]
        there.append(row_factor(matrix[:, order]))
        back.append(row_factor(matrix[:, order].T))
    by_line = matrix.reshape(NG, HALF, 2).transpose(0, 2, 1).reshape(NG, NG)
    return [jnp.asarray(value) for value in (
        kernel_table(), np.stack(there), np.stack(back),
        row_factor(by_line), row_factor(by_line.T), lane_factor(matrix),
    )]


def solve(pieces, partner, fixed):
    groups = len(pieces)
    count, rows, square = pieces[0].shape
    block = pl.BlockSpec((1, rows, square), lambda i: (i, 0, 0))
    whole = lambda array: pl.BlockSpec(array.shape, lambda i: (0,) * array.ndim)
    fixed = (partner,) + tuple(fixed)
    return pl.pallas_call(
        lambda *refs: solve_body(groups, *refs),
        grid=(count,),
        in_specs=[block] * groups + [whole(a) for a in fixed],
        out_specs=[block] * groups,
        out_shape=[jax.ShapeDtypeStruct(p.shape, BF) for p in pieces],
        scratch_shapes=[pltpu.VMEM((NG * HALF, LANES), F32)],
        compiler_params=pltpu.CompilerParams(vmem_limit_bytes=32 * 1024 * 1024),
        cost_estimate=pl.CostEstimate(
            flops=count * 12 * NG * NG * NG * 256, bytes_accessed=4 * count * NPTS, transcendentals=0
        ),
    )(*pieces, *fixed)
def swap_into(held, keep, send):
    width = held.shape[2] // 2
    mine = lax.axis_index("band") % 2

    @pl.loop(0, width // SWAP)
    def _(i):
        put = pl.ds(pl.multiple_of(i * SWAP, SWAP), SWAP)
        for at, out in ((mine, keep), (1 - mine, send)):
            lanes = pl.ds(pl.multiple_of(at * width + i * SWAP, SWAP), SWAP)
            out[:, :, put] = jnp.swapaxes(held[:, :, lanes], 0, 1)


def order_orbitals(orbitals):
    bands, rows, square = orbitals.shape
    part = jax.ShapeDtypeStruct((rows, bands, square // 2), BF)
    spec = pl.BlockSpec((rows, TILE, square // 2), lambda i: (0, i, 0))
    return pl.pallas_call(
        swap_into,
        grid=(bands // TILE,),
        in_specs=[pl.BlockSpec((TILE, rows, square), lambda i: (i, 0, 0))],
        out_specs=[spec] * 2,
        out_shape=[part] * 2,
        compiler_params=pltpu.CompilerParams(vmem_limit_bytes=24 * 1024 * 1024),
        cost_estimate=pl.CostEstimate(flops=0, bytes_accessed=4 * orbitals.size, transcendentals=0),
    )(orbitals)


def whole_body(chunks, groups, *refs):
    (orb, slab, okeep, osend, table, x_there, x_back, y_there, y_back, z_both,
     vectors, opeer, slots, extra, gram,
     cubes, solved, fresh, partner, hyper, ekeep, epeer, esend, lslots, work, obuf, abuf,
     parts, turned, sums, come, last,
     hyper_sem, pick_sem, fwd_sem, own_sem, back_sem, stay_sem, out_sem,
     oy_sem, r_sem, c_sem, ey_sem, l_sem, load_sem, sum_sem, last_sem) = refs
    count, rows = cubes.shape[2:4]
    low = lslots.shape[3]
    high = rows - low
    more = extra.shape[1]
    band, me = lax.axis_index("band"), lax.axis_index("grid")
    layer, line = band // 2, band % 2
    peer = band ^ 1
    up, down = lax.rem(band + 2, 8), lax.rem(band + 6, 8)

    def remote(source, target, sems, axis, index):
        return pltpu.make_async_remote_copy(
            src_ref=source, dst_ref=target, send_sem=sems[0], recv_sem=sems[1],
            device_id={axis: index}, device_id_type=pl.DeviceIdType.MESH,
        )

    def sems(array, *at):
        return array.at[(0,) + at], array.at[(1,) + at]

    def start(moves):
        for move in moves:
            move.start()

    def arrive(moves):
        for move in moves:
            move.wait_recv()

    def leave(moves):
        for move in moves:
            move.wait_send()

    def on(*layers):
        hit = layer == layers[0]
        for other in layers[1:]:
            hit = hit | (layer == other)
        return pl.when(hit)

    barrier = pltpu.get_barrier_semaphore()
    for bits in range(1, 8):
        pl.semaphore_signal(barrier, inc=1, device_id={"band": band ^ bits}, device_id_type=pl.DeviceIdType.MESH)
    for d in range(1, groups):
        pl.semaphore_signal(barrier, inc=1, device_id={"grid": me ^ d}, device_id_type=pl.DeviceIdType.MESH)
    pl.semaphore_wait(barrier, 6 + groups)

    def forward(c):
        def at(d):
            return orb.at[pl.ds(c * TILE + (me ^ d) * count, count)]
        moves = [remote(at(d), cubes.at[c, d], sems(fwd_sem, c, d - 1), "grid", me ^ d) for d in range(1, groups)]
        return moves, pltpu.make_async_copy(at(0), cubes.at[c, 0], own_sem.at[c])

    def start_forward(c):
        moves, stay = forward(c)
        start(moves)
        stay.start()

    def wait_forward(c):
        moves, stay = forward(c)
        arrive(moves)
        stay.wait()

    def back(c, mine):
        def at(d):
            return fresh.at[c, pl.ds((me if mine else me ^ d) * count, count)]
        moves = [remote(solved.at[c % 2, d], at(d), sems(back_sem, c, d - 1), "grid", me ^ d) for d in range(1, groups)]
        own = fresh.at[c, pl.ds(me * count, count)]
        return moves, pltpu.make_async_copy(solved.at[c % 2, 0], own, stay_sem.at[c])

    def start_back(c):
        moves, stay = back(c, True)
        start(moves)
        stay.start()

    def free_solved(c):
        leave(back(c, True)[0])

    low_cut = ((0, (low + 1) // 2), ((low + 1) // 2, low // 2))
    high_cut = ((0, (high + 1) // 2), ((high + 1) // 2, high // 2))

    def r_move(slot, side, q, source, first=0, cut=low_cut):
        at, size = cut[q]
        return remote(
            source.at[pl.ds(first + at, size)], slots.at[slot, side, pl.ds(at, size)],
            sems(r_sem, slot, side, q), "band", up,
        )

    def r_pass(slot, side, q, onto):
        return r_move(onto, side, q, slots.at[slot, side])

    def r_here(slot, side, q, cut=low_cut):
        return r_move(slot, side, q, slots.at[slot, side], 0, cut)

    def c_move(side, source):
        return remote(source.at[pl.ds(0, more)], extra.at[side], sems(c_sem, side), "band", up)

    def l_move(slot, side, c, source, first, size):
        return remote(
            source.at[pl.ds(first, size)], lslots.at[slot, side, c, pl.ds(0, size)],
            sems(l_sem, slot, side, c), "band", down,
        )

    def l_here(slot, side, c, size=high):
        return l_move(slot, side, c, lslots.at[slot, side, c], 0, size)

    def oy(half):
        at = pl.ds(low, high) if half else pl.ds(0, low)
        return remote(osend.at[at], opeer.at[at], sems(oy_sem, half), "band", peer)

    def ey(c, half):
        at = pl.ds(low, high) if half else pl.ds(0, low)
        return remote(esend.at[c, at], epeer.at[c, at], sems(ey_sem, c, half), "band", peer)

    steps = [remote(slab, hyper.at[0], sems(hyper_sem, 0), "band", band ^ 1)]
    steps.append(remote(hyper.at[3], hyper.at[1], sems(hyper_sem, 1), "band", band ^ 2))
    steps.append(remote(hyper.at[4], hyper.at[2], sems(hyper_sem, 2), "band", band ^ 4))
    mine = pl.ds(0, rows)
    picks = [
        remote(partner.at[mine], partner.at[pl.ds(d * rows, rows)], sems(pick_sem, d - 1), "grid", me ^ d)
        for d in range(1, groups)
    ]
    steps[0].start()
    start_forward(0)
    steps[0].wait_recv()
    hyper[3] = slab[...] + hyper[0]
    steps[1].start()
    oy(0).start()
    steps[1].wait_recv()
    hyper[4] = hyper[3] + hyper[1]
    steps[2].start()

    @on(0, 1)
    def _():
        start([r_move(0, 0, q, okeep) for q in range(2)])

    @on(2)
    def _():
        c_move(0, okeep).start()

    steps[2].wait_recv()
    partner[mine] = hyper[4] + hyper[2]
    start(picks)
    start_forward(1)
    oy(1).start()

    def own_orbitals(q):
        @on(1)
        def _():
            r_here(0, 0, q).wait_recv()
            r_pass(0, 0, q, 1).start()

        @on(2)
        def _():
            r_here(0, 0, q).wait_recv()
            r_pass(0, 0, q, 0).start()

        @on(0)
        def _():
            r_move(1, 0, q, okeep, low, high_cut).start()

    def own_orbitals_on(q):
        @on(2)
        def _():
            r_here(1, 0, q).wait_recv()
            r_pass(1, 0, q, 1).start()

        if q == 0:
            oy(0).wait_recv()

            @on(0, 1)
            def _():
                start([r_move(0, 1, part, opeer) for part in range(2)])

            @on(2)
            def _():
                c_move(1, opeer).start()

    def peer_orbitals(q):
        if q == 0:
            oy(1).wait_recv()

        @on(1)
        def _():
            r_here(0, 1, q).wait_recv()
            r_pass(0, 1, q, 1).start()

        @on(2)
        def _():
            r_here(0, 1, q).wait_recv()
            r_pass(0, 1, q, 0).start()

        @on(0)
        def _():
            r_move(1, 1, q, opeer, low, high_cut).start()

    def peer_orbitals_on(q):
        @on(2)
        def _():
            r_here(1, 1, q).wait_recv()
            r_pass(1, 1, q, 1).start()

    def out_move(c):
        return pltpu.make_async_copy(fresh.at[c], vectors.at[pl.ds(c * TILE, TILE)], out_sem.at[c])

    def collect(c):
        moves, stay = back(c, False)
        arrive(moves)
        stay.wait()
        out_move(c).start()
        swap_into(fresh.at[c], ekeep.at[c], esend.at[c])
        ey(c, 1).start()
        send_vectors(c, 0)
        ey(c, 0).start()

    def send_vectors(c, side):
        source = (epeer if side else ekeep).at[c]
        if side:
            ey(c, 1).wait_recv()

        @on(2, 3)
        def _():
            l_move(0, side, c, source, low, high).start()

        if side:
            ey(c, 0).wait_recv()

        @on(3)
        def _():
            l_move(1, side, c, source, more, low - more).start()

    def pass_first(c, side):
        @on(2)
        def _():
            l_here(0, side, c).wait_recv()
            l_move(1, side, c, lslots.at[0, side, c], 0, high).start()

        @on(1)
        def _():
            l_here(0, side, c).wait_recv()
            l_move(0, side, c, lslots.at[0, side, c], 0, high).start()

    def pass_second(c, side):
        @on(1)
        def _():
            l_here(1, side, c).wait_recv()
            l_move(1, side, c, lslots.at[1, side, c], 0, high).start()

    arrive(picks)
    before = {
        0: [(wait_forward, 0)],
        4: [(wait_forward, 1)],
        8: [(pass_first, 0, 0), (own_orbitals_on, 0), (wait_forward, 2), (free_solved, 0)],
        12: [(pass_second, 0, 1), (pass_first, 1, 0), (wait_forward, 3), (free_solved, 1)],
    }
    after = {
        0: [(own_orbitals, 0)],
        3: [(start_back, 0)],
        4: [(own_orbitals, 1)],
        5: [(start_forward, 2)],
        7: [(start_back, 1), (collect, 0)],
        8: [(pass_second, 0, 0)],
        9: [(start_forward, 3), (send_vectors, 0, 1)],
        11: [(start_back, 2), (pass_first, 0, 1), (own_orbitals_on, 1), (collect, 1)],
        12: [(send_vectors, 1, 1), (pass_second, 1, 0)],
        13: [(peer_orbitals, 0)],
        15: [(start_back, 3), (pass_first, 1, 1), (collect, 2)],
    }

    def run(events):
        for event in events:
            event[0](*event[1:])

    def at_slot(t, table):
        for slot, events in table.items():
            @pl.when(t == slot)
            def _():
                run(events)

    @pl.loop(0, chunks * count)
    def _(t):
        at_slot(t, before)
        c, j = t // count, lax.rem(t, count)
        solve_one(
            [cubes.at[c, d, j] for d in range(groups)], partner, table, x_there, x_back,
            y_there, y_back, z_both, [solved.at[lax.rem(c, 2), d, j] for d in range(groups)], work,
        )
        at_slot(t, after)

    run((
        (pass_second, 1, 1), (peer_orbitals, 1), (pass_first, 2, 0), (send_vectors, 2, 1), (pass_second, 2, 0),
        (peer_orbitals_on, 0), (pass_first, 2, 1), (collect, 3), (pass_second, 2, 1),
        (peer_orbitals_on, 1), (pass_first, 3, 0), (send_vectors, 3, 1), (pass_second, 3, 0),
    ))

    sides = [(side, c) for side in range(2) for c in range(chunks)]

    def loads(p, at):
        return [
            pltpu.make_async_copy(source.at[p], obuf.at[at, side], load_sem.at[at, side])
            for side, source in enumerate((okeep, opeer))
        ]

    def slot_loads(slot, p, at):
        return [
            pltpu.make_async_copy(slots.at[slot, side, p], abuf.at[at, slot, side], load_sem.at[at, 2 + slot * 2 + side])
            for side in range(2)
        ]

    def extra_loads(p, at):
        return [
            pltpu.make_async_copy(extra.at[side, p], abuf.at[at, 1, side], load_sem.at[at, 4 + side])
            for side in range(2)
        ]

    def early_slots(p, at, act):
        @pl.when((layer > 0) & (p < low))
        def _():
            act(1, slot_loads(0, p, at), 0)

        @pl.when((layer == 2) & (p < low))
        def _():
            act(2, slot_loads(1, p, at), 1)

        @pl.when((layer == 1) & (p >= low))
        def _():
            act(2, slot_loads(1, p - low, at), 1)

        @pl.when((layer == 3) & (p < more))
        def _():
            act(5, extra_loads(p, at), 1)

    def late_slots(p, at, act):
        @pl.when((layer == 3) & (p < low))
        def _():
            act(2, slot_loads(1, p, at), 1)

    def across(a, b):
        return lax.dot_general(a, b, (((1,), (1,)), ((), ())), preferred_element_type=F32)

    def rows_of(buffer):
        return jnp.concatenate([buffer[side] for side in range(2)], axis=0)

    def own_rows(p):
        return jnp.concatenate([ref[c, p] for ref in (ekeep, epeer) for c in range(chunks)], axis=0)

    def in_turn(first, last, load, use):
        load(first, first % 2, lambda index, moves, slot: start(moves))

        @pl.loop(first, last)
        def _(p):
            at = lax.rem(p, 2)

            @pl.when(p + 1 < last)
            def _():
                load(p + 1, 1 - at, lambda index, moves, slot: start(moves))

            use(p, at)

    def with_own(slots_of):
        def load(p, at, act):
            act(0, loads(p, at), None)
            slots_of(p, at, act)
        return load

    def early(p, at):
        there = own_rows(p)
        for move in loads(p, at):
            move.wait()
        parts[0] += across(rows_of(obuf.at[at]), there)

        def add(index, moves, slot):
            for move in moves:
                move.wait()
            parts[index] += across(rows_of(abuf.at[at, slot]), there)

        early_slots(p, at, add)

    def late(p, at):
        for move in loads(p, at):
            move.wait()
        here = rows_of(obuf.at[at])

        def add(index, moves, slot):
            for move in moves:
                move.wait()
            parts[index] += across(rows_of(abuf.at[at, slot]), own_rows(p))

        late_slots(p, at, add)

        def moved(slot, plane):
            parts[3 + slot] += across(here, jnp.concatenate([lslots[slot, side, c, plane] for side, c in sides], axis=0))

        @pl.when((layer < 3) & (p >= low))
        def _():
            moved(0, p - low)

        @pl.when((layer < 2) & (p >= low))
        def _():
            moved(1, p - low)

        @pl.when((layer == 2) & (p >= more) & (p < low))
        def _():
            moved(1, p - more)

    parts[...] = jnp.zeros_like(parts)
    @on(1)
    def _():
        for side in range(2):
            arrive([r_here(1, side, q, high_cut) for q in range(2)])

    @on(3)
    def _():
        for side in range(2):
            arrive([r_here(0, side, q) for q in range(2)] + [c_move(side, extra.at[side])])

    in_turn(0, rows, with_own(early_slots), early)
    run(((pass_first, 3, 1), (pass_second, 3, 1)))

    @on(0)
    def _():
        for side, c in sides:
            arrive([l_here(slot, side, c) for slot in range(2)])

    @on(2)
    def _():
        for side, c in sides:
            l_here(1, side, c, low - more).wait_recv()

    @on(3)
    def _():
        for side in range(2):
            arrive([r_here(1, side, q) for q in range(2)])

    in_turn(0, rows, with_own(late_slots), late)

    size = parts.shape[1]
    half = size // 2
    for at in range(chunks):
        @on(at)
        def _():
            for other in range(chunks):
                if other == at:
                    turned[other] = parts[0]
                else:
                    found = [parts[i] if i in (3, 4) else parts[i].T for i in HELD[at].get(other, ())]
                    turned[other] = sum(found[1:], found[0]) if found else jnp.zeros((size, size), F32)
    for other in range(chunks):
        block = turned[other] * (1.0 / NPTS)
        block = jnp.where(line == 1, pltpu.roll(block, half, 1), block)
        sums[0, other] = block[half:]
        sums[1, other] = block[:half]
    totals = [
        remote(sums.at[0], come.at[0], sems(sum_sem, 0), "band", peer),
        remote(sums.at[2], come.at[1], sems(sum_sem, 1), "grid", me ^ 1),
        remote(sums.at[3], come.at[2], sems(sum_sem, 2), "grid", me ^ 2),
    ]
    for i, move in enumerate(totals):
        move.start()
        move.wait_recv()
        sums[2 + i] = sums[1 + i] + come[i]
    swaps = []
    for bits in range(1, chunks):
        block = sums.at[4, layer ^ bits]
        for turn in range(2):
            swaps.append((remote(
                block, last.at[bits - 1, line], sems(last_sem, bits - 1, turn), "band", band ^ (2 * bits + turn)
            ), remote(
                block, last.at[bits - 1, line ^ turn], sems(last_sem, bits - 1, turn), "band", band ^ (2 * bits + turn)
            )))
    for move, _ in swaps:
        move.start()
    gram[:, pl.ds(pl.multiple_of(layer * size, size), size)] = sums[4, layer]
    for _, move in swaps:
        move.wait_recv()
    for bits in range(1, chunks):
        whole_block = jnp.concatenate([last[bits - 1, 0], last[bits - 1, 1]], axis=0).T
        mine_block = jnp.where(line == 0, whole_block[:half], whole_block[half:])
        there = layer ^ bits
        gram[:, pl.ds(pl.multiple_of(there * size, size), size)] = sums[4, there] + mine_block

    leave(steps + picks + totals + [move for move, _ in swaps] + [oy(half) for half in range(2)])

    for c in range(chunks):
        out_move(c).wait()
        leave([ey(c, half) for half in range(2)] + forward(c)[0])
        if c >= chunks - 2:
            leave(back(c, True)[0])

    @on(0)
    def _():
        for side in range(2):
            leave([r_here(0, side, q) for q in range(2)] + [r_here(1, side, q, high_cut) for q in range(2)])

    @on(2)
    def _():
        leave([c_move(side, extra.at[side]) for side in range(2)])

    @on(1, 2)
    def _():
        for side in range(2):
            leave([r_here(slot, side, q) for slot in range(2) for q in range(2)])

    @on(1, 2, 3)
    def _():
        for side, c in sides:
            l_here(0, side, c).wait_send()

    @on(1, 2)
    def _():
        for side, c in sides:
            l_here(1, side, c).wait_send()

    @on(3)
    def _():
        for side, c in sides:
            l_here(1, side, c, low - more).wait_send()


def whole(orbitals, slab, okeep, osend, fixed):
    bands, rows, square = orbitals.shape
    groups = lax.axis_size("grid")
    chunks, count = bands // TILE, TILE // groups
    low, width = LOW * rows // 16, square // 2
    anywhere = pl.BlockSpec(memory_space=pl.ANY)
    inside = pl.BlockSpec(memory_space=pltpu.VMEM)
    dma = pltpu.SemaphoreType.DMA
    size = 2 * bands
    return pl.pallas_call(
        lambda *refs: whole_body(chunks, groups, *refs),
        in_specs=[anywhere, inside, anywhere, anywhere] + [inside] * len(fixed),
        out_specs=[anywhere] * 4 + [inside],
        out_shape=[
            jax.ShapeDtypeStruct(orbitals.shape, BF),
            jax.ShapeDtypeStruct((rows, bands, width), BF),
            jax.ShapeDtypeStruct((2, 2, low, bands, width), BF),
            jax.ShapeDtypeStruct((2, MORE, bands, width), BF),
            jax.ShapeDtypeStruct((bands, 4 * size), F32),
        ],
        scratch_shapes=[
            pltpu.VMEM((chunks, groups, count, rows, square), BF),
            pltpu.VMEM((2, groups, count, rows, square), BF),
            pltpu.VMEM((chunks, TILE, rows, square), BF),
            pltpu.VMEM((NG, square), BF),
            pltpu.VMEM((5, rows, square), BF),
            pltpu.VMEM((chunks, rows, TILE, width), BF),
            pltpu.VMEM((chunks, rows, TILE, width), BF),
            pltpu.VMEM((chunks, rows, TILE, width), BF),
            pltpu.VMEM((2, 2, chunks, low, TILE, width), BF),
            pltpu.VMEM((NG * HALF, LANES), F32),
            pltpu.VMEM((2, 2, bands, width), BF),
            pltpu.VMEM((2, 2, 2, bands, width), BF),
            pltpu.VMEM((6, size, size), F32),
            pltpu.VMEM((4, size, size), F32),
            pltpu.VMEM((5, 4, bands, size), F32),
            pltpu.VMEM((3, 4, bands, size), F32),
            pltpu.VMEM((3, 2, bands, size), F32),
            dma((2, 3)), dma((2, groups - 1)), dma((2, chunks, groups - 1)), dma((chunks,)),
            dma((2, chunks, groups - 1)), dma((chunks,)), dma((chunks,)),
            dma((2, 2)), dma((2, 2, 2, 2)), dma((2, 2)), dma((2, chunks, 2)), dma((2, 2, 2, chunks)), dma((2, 6)),
            dma((2, 3)), dma((2, 3, 2)),
        ],
        compiler_params=pltpu.CompilerParams(
            collective_id=0, has_side_effects=True, vmem_limit_bytes=60 * 1024 * 1024
        ),
        cost_estimate=pl.CostEstimate(
            flops=chunks * count * 12 * NG * NG * NG * 256, bytes_accessed=16 * orbitals.size, transcendentals=0
        ),
    )(orbitals, slab, okeep, osend, *fixed)


def flip(value, axis, bits):
    return lax.ppermute(value, axis, [(i, i ^ bits) for i in range(lax.axis_size(axis))])


def gram_body(left, right, out):
    @pl.when(pl.program_id(0) == 0)
    def _():
        out[...] = jnp.zeros_like(out)

    size = out.shape[0]
    a = left[:, 0].reshape(size, left.shape[3])
    b = right[:, 0].reshape(size, right.shape[3])
    out[...] += lax.dot_general(a, b, (((1,), (1,)), ((), ())), preferred_element_type=F32)


def gram_product(left, right):
    shares, planes, bands, points = left.shape
    size = shares * bands
    if bands % 16 or points % 128:
        return jnp.einsum("gxbk,hxck->gbhc", left, right, preferred_element_type=F32).reshape(size, size)
    block = pl.BlockSpec((shares, 1, bands, points), lambda i: (0, i, 0, 0))
    return pl.pallas_call(
        gram_body,
        grid=(planes,),
        in_specs=[block, block],
        out_specs=pl.BlockSpec((size, size), lambda i: (0, 0)),
        out_shape=jax.ShapeDtypeStruct((size, size), F32),
        compiler_params=pltpu.CompilerParams(vmem_limit_bytes=32 * 1024 * 1024),
        cost_estimate=pl.CostEstimate(
            flops=2 * size * size * planes * points, bytes_accessed=4 * left.size, transcendentals=0
        ),
    )(left, right)


def to_shares(array):
    shares = lax.axis_size("band")
    bands, planes, square = array.shape
    cut = array.reshape(bands, planes, shares, square // shares).transpose(2, 1, 0, 3)
    return lax.all_to_all(cut, "band", split_axis=0, concat_axis=0)


def spread(slab):
    bit = 1
    while bit < lax.axis_size("band"):
        slab = slab + flip(slab, "band", bit)
        bit *= 2
    groups = lax.axis_size("grid")
    return jnp.concatenate([slab] + [flip(slab, "grid", d) for d in range(1, groups)], axis=0)


def per_device(orbitals, picks):
    bands, planes, square = orbitals.shape
    groups, shares = lax.axis_size("grid"), lax.axis_size("band")
    me = lax.axis_index("grid")
    fixed = factors(groups)
    target = picks[0]
    mine = lax.dynamic_index_in_dim(orbitals, target % bands, 0, keepdims=False)
    slab = jnp.where(lax.axis_index("band") == target // bands, mine, 0).astype(BF)

    if shares == 8 and groups == 4 and bands == 4 * TILE and planes == 16:
        vectors, _, _, _, gram = whole(orbitals, slab, *order_orbitals(orbitals), fixed)
        return (vectors, gram)

    partner = spread(slab)
    count = bands // groups
    pieces = []
    for d in range(groups):
        part = lax.dynamic_slice_in_dim(orbitals, (me ^ d) * count, count, 0)
        pieces.append(flip(part, "grid", d) if d else part)
    solved = solve(pieces, partner, fixed)
    back = [flip(p, "grid", d) if d else p for d, p in enumerate(solved)]
    stacked = jnp.take(jnp.stack(back), me ^ jnp.arange(groups), axis=0)
    vectors = stacked.reshape(bands, planes, square)
    product = gram_product(to_shares(orbitals), to_shares(vectors))
    rows = lax.psum_scatter(product * (1.0 / NPTS), "band", scatter_dimension=0, tiled=True)
    return (vectors, lax.psum(rows, "grid"))


def solution(mesh):
    return jax.shard_map(
        per_device,
        mesh=mesh,
        in_specs=(P("band", "grid", None), P()),
        out_specs=(P("band", "grid", None), P("band", None)),
        check_vma=False,
    )
```

```python
import math
import jax
import jax.numpy as jnp
import ml_dtypes
import numpy as np
from jax import lax
from jax.experimental import pallas as pl
from jax.experimental.pallas import tpu as pltpu
from jax.sharding import PartitionSpec as P

NG = 64
NPTS = NG ** 3
KERNEL_SCALE = 128.0
LANES = 128
BF = ml_dtypes.bfloat16
F32 = jnp.float32
HALF = NG // 2
XW = 512
PLANES = 32
TILE = 16
SWAP = 256
LOW = 9
MORE = 3
HELD = ({2: (3,), 3: (4,)}, {0: (1, 2), 2: (3,), 3: (4,)}, {1: (1,), 0: (2,), 3: (3, 4)}, {1: (1,), 0: (2,), 2: (5,)})


def cas_matrix(length):
    products = np.arange(length)[:, None] * np.arange(length)[None, :] % length
    angles = products * (2.0 * math.pi / length)
    return (np.cos(angles) + np.sin(angles)).astype(np.float32)


def halves(value):
    high = value.astype(BF)
    return high, (value - high.astype(F32)).astype(BF)


def kernel_table():
    frequency = np.arange(NG)
    folded = np.minimum(frequency, NG - frequency)
    square = folded * folded
    summed = square[:, None, None] + square[None, :, None] + square[None, None, :]
    table = np.where(summed > 0, KERNEL_SCALE / NPTS / np.maximum(summed, 1), 0.0).astype(np.float32)
    return table.reshape(NG // 4, 4, NG, NG).transpose(0, 2, 1, 3).reshape(NG // 4, NG, 4 * NG)


def row_factor(matrix):
    high, low = halves(matrix)
    return np.concatenate([high, high, low], axis=1)


def lane_factor(matrix):
    high, low = halves(np.kron(np.eye(2, dtype=np.float32), matrix))
    upper = np.concatenate([high, low], axis=1)
    lower = np.concatenate([high, np.zeros_like(low)], axis=1)
    return np.concatenate([upper, lower], axis=0)


def dot(a, b):
    return jnp.dot(a, b, preferred_element_type=F32)


def solve_one(ins, partner, table, x_there, x_back, y_there, y_back, z_both, outs, work):
    rows = NG // len(ins)
    me = lax.axis_index("grid")
    x_there, x_back = x_there.at[me], x_back.at[me]

    def along_rows(factor, value):
        high, low = halves(value)
        return dot(factor[...], jnp.concatenate([high, low, high], axis=0))

    def along_lanes(value):
        high, low = halves(value)
        both = dot(jnp.concatenate([high, low], axis=1), z_both[...])
        return both[:, :LANES] + both[:, LANES:]

    @pl.loop(0, NG * NG // XW, unroll=4)
    def _(i):
        at = pl.ds(pl.multiple_of(i * XW, XW), XW)
        field = jnp.concatenate([ref[:, at].astype(F32) for ref in ins], axis=0)
        field = along_rows(x_there, field * partner[:, at].astype(F32))
        for tile in range(XW // LANES):
            work[pl.ds(i * (XW // LANES) + tile, NG, stride=HALF), :] = field[:, tile * LANES:(tile + 1) * LANES]

    @pl.loop(0, NG // PLANES, unroll=2)
    def _(i):
        left = lax.broadcasted_iota(jnp.int32, (HALF, LANES), 1) < NG
        base = i * PLANES * HALF
        parts = []
        for pair in range(PLANES // 2):
            a = work[pl.ds(base + pair * NG, HALF), :]
            b = work[pl.ds(base + pair * NG + HALF, HALF), :]
            parts.append(jnp.where(left, a, pltpu.roll(b, NG, 1)))
            parts.append(jnp.where(left, pltpu.roll(a, NG, 1), b))
        field = along_lanes(jnp.concatenate(parts, axis=0))
        done = []
        for quad in range(PLANES // 4):
            wide = jnp.concatenate(
                [field[quad * 128:quad * 128 + 64], field[quad * 128 + 64:quad * 128 + 128]], axis=1
            )
            wide = along_rows(y_there, wide) * table[i * (PLANES // 4) + quad]
            wide = along_rows(y_back, wide)
            done.append(wide[:, :LANES])
            done.append(wide[:, LANES:])
        field = along_lanes(jnp.concatenate(done, axis=0))
        for pair in range(PLANES // 2):
            u = field[pair * NG:pair * NG + HALF]
            v = field[pair * NG + HALF:pair * NG + NG]
            work[pl.ds(base + pair * NG, HALF), :] = jnp.where(left, u, pltpu.roll(v, NG, 1))
            work[pl.ds(base + pair * NG + HALF, HALF), :] = jnp.where(left, pltpu.roll(u, NG, 1), v)

    @pl.loop(0, NG * NG // XW, unroll=4)
    def _(i):
        at = pl.ds(pl.multiple_of(i * XW, XW), XW)
        field = jnp.concatenate(
            [work[pl.ds(i * (XW // LANES) + tile, NG, stride=HALF), :] for tile in range(XW // LANES)], axis=1
        )
        field = (-along_rows(x_back, field) * partner[:, at].astype(F32)).astype(BF)
        for index, ref in enumerate(outs):
            ref[:, at] = field[index * rows:(index + 1) * rows]


def solve_body(groups, *refs):
    ins, outs = refs[:groups], refs[groups + 7:2 * groups + 7]
    solve_one([ref.at[0] for ref in ins], *refs[groups:groups + 7], [ref.at[0] for ref in outs], refs[-1])


def factors(groups):
    matrix = cas_matrix(NG)
    there, back = [], []
    for me in range(groups):
        order = [slab * (NG // groups) + plane for slab in (me ^ d for d in range(groups)) for plane in range(NG // groups)]
        there.append(row_factor(matrix[:, order]))
        back.append(row_factor(matrix[:, order].T))
    by_line = matrix.reshape(NG, HALF, 2).transpose(0, 2, 1).reshape(NG, NG)
    return [jnp.asarray(value) for value in (
        kernel_table(), np.stack(there), np.stack(back),
        row_factor(by_line), row_factor(by_line.T), lane_factor(matrix),
    )]


def solve(pieces, partner, fixed):
    groups = len(pieces)
    count, rows, square = pieces[0].shape
    block = pl.BlockSpec((1, rows, square), lambda i: (i, 0, 0))
    whole = lambda array: pl.BlockSpec(array.shape, lambda i: (0,) * array.ndim)
    fixed = (partner,) + tuple(fixed)
    return pl.pallas_call(
        lambda *refs: solve_body(groups, *refs),
        grid=(count,),
        in_specs=[block] * groups + [whole(a) for a in fixed],
        out_specs=[block] * groups,
        out_shape=[jax.ShapeDtypeStruct(p.shape, BF) for p in pieces],
        scratch_shapes=[pltpu.VMEM((NG * HALF, LANES), F32)],
        compiler_params=pltpu.CompilerParams(vmem_limit_bytes=32 * 1024 * 1024),
        cost_estimate=pl.CostEstimate(
            flops=count * 12 * NG * NG * NG * 256, bytes_accessed=4 * count * NPTS, transcendentals=0
        ),
    )(*pieces, *fixed)
def swap_into(held, keep, send):
    width = held.shape[2] // 2
    mine = lax.axis_index("band") % 2

    @pl.loop(0, width // SWAP)
    def _(i):
        put = pl.ds(pl.multiple_of(i * SWAP, SWAP), SWAP)
        for at, out in ((mine, keep), (1 - mine, send)):
            lanes = pl.ds(pl.multiple_of(at * width + i * SWAP, SWAP), SWAP)
            out[:, :, put] = jnp.swapaxes(held[:, :, lanes], 0, 1)


def order_orbitals(orbitals):
    bands, rows, square = orbitals.shape
    part = jax.ShapeDtypeStruct((rows, bands, square // 2), BF)
    spec = pl.BlockSpec((rows, TILE, square // 2), lambda i: (0, i, 0))
    return pl.pallas_call(
        swap_into,
        grid=(bands // TILE,),
        in_specs=[pl.BlockSpec((TILE, rows, square), lambda i: (i, 0, 0))],
        out_specs=[spec] * 2,
        out_shape=[part] * 2,
        compiler_params=pltpu.CompilerParams(vmem_limit_bytes=60 * 1024 * 1024),
        cost_estimate=pl.CostEstimate(flops=0, bytes_accessed=4 * orbitals.size, transcendentals=0),
    )(orbitals)


def whole_body(chunks, groups, *refs):
    (orb, slab, okeep, osend, table, x_there, x_back, y_there, y_back, z_both,
     vectors, opeer, slots, extra, gram,
     cubes, solved, fresh, partner, hyper, ekeep, epeer, esend, lslots, work, obuf, abuf,
     parts, turned, sums, come, last,
     hyper_sem, pick_sem, fwd_sem, own_sem, back_sem, stay_sem, out_sem,
     oy_sem, r_sem, c_sem, ey_sem, l_sem, load_sem, sum_sem, last_sem) = refs
    count, rows = cubes.shape[2:4]
    low = lslots.shape[3]
    high = rows - low
    more = extra.shape[1]
    band, me = lax.axis_index("band"), lax.axis_index("grid")
    layer, line = band // 2, band % 2
    peer = band ^ 1
    up, down = lax.rem(band + 2, 8), lax.rem(band + 6, 8)

    def remote(source, target, sems, axis, index):
        return pltpu.make_async_remote_copy(
            src_ref=source, dst_ref=target, send_sem=sems[0], recv_sem=sems[1],
            device_id={axis: index}, device_id_type=pl.DeviceIdType.MESH,
        )

    def sems(array, *at):
        return array.at[(0,) + at], array.at[(1,) + at]

    def start(moves):
        for move in moves:
            move.start()

    def arrive(moves):
        for move in moves:
            move.wait_recv()

    def leave(moves):
        for move in moves:
            move.wait_send()

    def on(*layers):
        hit = layer == layers[0]
        for other in layers[1:]:
            hit = hit | (layer == other)
        return pl.when(hit)

    barrier = pltpu.get_barrier_semaphore()
    for bits in range(1, 8):
        pl.semaphore_signal(barrier, inc=1, device_id={"band": band ^ bits}, device_id_type=pl.DeviceIdType.MESH)
    for d in range(1, groups):
        pl.semaphore_signal(barrier, inc=1, device_id={"grid": me ^ d}, device_id_type=pl.DeviceIdType.MESH)
    pl.semaphore_wait(barrier, 6 + groups)

    def forward(c):
        def at(d):
            return orb.at[pl.ds(c * TILE + (me ^ d) * count, count)]
        moves = [remote(at(d), cubes.at[c, d], sems(fwd_sem, c, d - 1), "grid", me ^ d) for d in range(1, groups)]
        return moves, pltpu.make_async_copy(at(0), cubes.at[c, 0], own_sem.at[c])

    def start_forward(c):
        moves, stay = forward(c)
        start(moves)
        stay.start()

    def wait_forward(c):
        moves, stay = forward(c)
        arrive(moves)
        stay.wait()

    def back(c, mine):
        def at(d):
            return fresh.at[c, pl.ds((me if mine else me ^ d) * count, count)]
        moves = [remote(solved.at[c % 2, d], at(d), sems(back_sem, c, d - 1), "grid", me ^ d) for d in range(1, groups)]
        own = fresh.at[c, pl.ds(me * count, count)]
        return moves, pltpu.make_async_copy(solved.at[c % 2, 0], own, stay_sem.at[c])

    def start_back(c):
        moves, stay = back(c, True)
        start(moves)
        stay.start()

    def free_solved(c):
        leave(back(c, True)[0])

    low_cut = ((0, (low + 1) // 2), ((low + 1) // 2, low // 2))
    high_cut = ((0, (high + 1) // 2), ((high + 1) // 2, high // 2))

    def r_move(slot, side, q, source, first=0, cut=low_cut):
        at, size = cut[q]
        return remote(
            source.at[pl.ds(first + at, size)], slots.at[slot, side, pl.ds(at, size)],
            sems(r_sem, slot, side, q), "band", up,
        )

    def r_pass(slot, side, q, onto):
        return r_move(onto, side, q, slots.at[slot, side])

    def r_here(slot, side, q, cut=low_cut):
        return r_move(slot, side, q, slots.at[slot, side], 0, cut)

    def c_move(side, source):
        return remote(source.at[pl.ds(0, more)], extra.at[side], sems(c_sem, side), "band", up)

    def l_move(slot, side, c, source, first, size):
        return remote(
            source.at[pl.ds(first, size)], lslots.at[slot, side, c, pl.ds(0, size)],
            sems(l_sem, slot, side, c), "band", down,
        )

    def l_here(slot, side, c, size=high):
        return l_move(slot, side, c, lslots.at[slot, side, c], 0, size)

    def oy(half):
        at = pl.ds(low, high) if half else pl.ds(0, low)
        return remote(osend.at[at], opeer.at[at], sems(oy_sem, half), "band", peer)

    def ey(c, half):
        at = pl.ds(low, high) if half else pl.ds(0, low)
        return remote(esend.at[c, at], epeer.at[c, at], sems(ey_sem, c, half), "band", peer)

    steps = [remote(slab, hyper.at[0], sems(hyper_sem, 0), "band", band ^ 1)]
    steps.append(remote(hyper.at[3], hyper.at[1], sems(hyper_sem, 1), "band", band ^ 2))
    steps.append(remote(hyper.at[4], hyper.at[2], sems(hyper_sem, 2), "band", band ^ 4))
    mine = pl.ds(0, rows)
    picks = [
        remote(partner.at[mine], partner.at[pl.ds(d * rows, rows)], sems(pick_sem, d - 1), "grid", me ^ d)
        for d in range(1, groups)
    ]
    steps[0].start()
    start_forward(0)
    steps[0].wait_recv()
    hyper[3] = slab[...] + hyper[0]
    steps[1].start()
    oy(0).start()
    steps[1].wait_recv()
    hyper[4] = hyper[3] + hyper[1]
    steps[2].start()

    @on(0, 1)
    def _():
        start([r_move(0, 0, q, okeep) for q in range(2)])

    @on(2)
    def _():
        c_move(0, okeep).start()

    steps[2].wait_recv()
    partner[mine] = hyper[4] + hyper[2]
    start(picks)
    start_forward(1)
    oy(1).start()

    def own_orbitals(q):
        @on(1)
        def _():
            r_here(0, 0, q).wait_recv()
            r_pass(0, 0, q, 1).start()

        @on(2)
        def _():
            r_here(0, 0, q).wait_recv()
            r_pass(0, 0, q, 0).start()

        @on(0)
        def _():
            r_move(1, 0, q, okeep, low, high_cut).start()

    def own_orbitals_on(q):
        @on(2)
        def _():
            r_here(1, 0, q).wait_recv()
            r_pass(1, 0, q, 1).start()

        if q == 0:
            oy(0).wait_recv()

            @on(0, 1)
            def _():
                start([r_move(0, 1, part, opeer) for part in range(2)])

            @on(2)
            def _():
                c_move(1, opeer).start()

    def peer_orbitals(q):
        if q == 0:
            oy(1).wait_recv()

        @on(1)
        def _():
            r_here(0, 1, q).wait_recv()
            r_pass(0, 1, q, 1).start()

        @on(2)
        def _():
            r_here(0, 1, q).wait_recv()
            r_pass(0, 1, q, 0).start()

        @on(0)
        def _():
            r_move(1, 1, q, opeer, low, high_cut).start()

    def peer_orbitals_on(q):
        @on(2)
        def _():
            r_here(1, 1, q).wait_recv()
            r_pass(1, 1, q, 1).start()

    def out_move(c):
        return pltpu.make_async_copy(fresh.at[c], vectors.at[pl.ds(c * TILE, TILE)], out_sem.at[c])

    def collect(c):
        moves, stay = back(c, False)
        arrive(moves)
        stay.wait()
        out_move(c).start()
        swap_into(fresh.at[c], ekeep.at[c], esend.at[c])
        ey(c, 1).start()
        send_vectors(c, 0)
        ey(c, 0).start()

    def send_vectors(c, side):
        source = (epeer if side else ekeep).at[c]
        if side:
            ey(c, 1).wait_recv()

        @on(2, 3)
        def _():
            l_move(0, side, c, source, low, high).start()

        if side:
            ey(c, 0).wait_recv()

        @on(3)
        def _():
            l_move(1, side, c, source, more, low - more).start()

    def pass_first(c, side):
        @on(2)
        def _():
            l_here(0, side, c).wait_recv()
            l_move(1, side, c, lslots.at[0, side, c], 0, high).start()

        @on(1)
        def _():
            l_here(0, side, c).wait_recv()
            l_move(0, side, c, lslots.at[0, side, c], 0, high).start()

    def pass_second(c, side):
        @on(1)
        def _():
            l_here(1, side, c).wait_recv()
            l_move(1, side, c, lslots.at[1, side, c], 0, high).start()

    arrive(picks)
    before = {
        0: [(wait_forward, 0)],
        4: [(wait_forward, 1)],
        8: [(pass_first, 0, 0), (own_orbitals_on, 0), (wait_forward, 2), (free_solved, 0)],
        12: [(pass_second, 0, 1), (pass_first, 1, 0), (wait_forward, 3), (free_solved, 1)],
    }
    after = {
        0: [(own_orbitals, 0)],
        3: [(start_back, 0)],
        4: [(own_orbitals, 1)],
        5: [(start_forward, 2)],
        7: [(start_back, 1), (collect, 0)],
        8: [(pass_second, 0, 0)],
        9: [(start_forward, 3), (send_vectors, 0, 1)],
        11: [(start_back, 2), (pass_first, 0, 1), (own_orbitals_on, 1), (collect, 1)],
        12: [(send_vectors, 1, 1), (pass_second, 1, 0)],
        13: [(peer_orbitals, 0)],
        15: [(start_back, 3), (pass_first, 1, 1), (collect, 2)],
    }

    def run(events):
        for event in events:
            event[0](*event[1:])

    def at_slot(t, table):
        for slot, events in table.items():
            @pl.when(t == slot)
            def _():
                run(events)

    @pl.loop(0, chunks * count)
    def _(t):
        at_slot(t, before)
        c, j = t // count, lax.rem(t, count)
        solve_one(
            [cubes.at[c, d, j] for d in range(groups)], partner, table, x_there, x_back,
            y_there, y_back, z_both, [solved.at[lax.rem(c, 2), d, j] for d in range(groups)], work,
        )
        at_slot(t, after)

    run((
        (pass_second, 1, 1), (peer_orbitals, 1), (pass_first, 2, 0), (send_vectors, 2, 1), (pass_second, 2, 0),
        (peer_orbitals_on, 0), (pass_first, 2, 1), (collect, 3), (pass_second, 2, 1),
        (peer_orbitals_on, 1), (pass_first, 3, 0), (send_vectors, 3, 1), (pass_second, 3, 0),
    ))

    sides = [(side, c) for side in range(2) for c in range(chunks)]

    def loads(p, at):
        return [
            pltpu.make_async_copy(source.at[p], obuf.at[at, side], load_sem.at[at, side])
            for side, source in enumerate((okeep, opeer))
        ]

    def slot_loads(slot, p, at):
        return [
            pltpu.make_async_copy(slots.at[slot, side, p], abuf.at[at, slot, side], load_sem.at[at, 2 + slot * 2 + side])
            for side in range(2)
        ]

    def extra_loads(p, at):
        return [
            pltpu.make_async_copy(extra.at[side, p], abuf.at[at, 1, side], load_sem.at[at, 4 + side])
            for side in range(2)
        ]

    def early_slots(p, at, act):
        @pl.when((layer > 0) & (p < low))
        def _():
            act(1, slot_loads(0, p, at), 0)

        @pl.when((layer == 2) & (p < low))
        def _():
            act(2, slot_loads(1, p, at), 1)

        @pl.when((layer == 1) & (p >= low))
        def _():
            act(2, slot_loads(1, p - low, at), 1)

        @pl.when((layer == 3) & (p < more))
        def _():
            act(5, extra_loads(p, at), 1)

    def late_slots(p, at, act):
        @pl.when((layer == 3) & (p < low))
        def _():
            act(2, slot_loads(1, p, at), 1)

    def across(a, b):
        return lax.dot_general(a, b, (((1,), (1,)), ((), ())), preferred_element_type=F32)

    def rows_of(buffer):
        return jnp.concatenate([buffer[side] for side in range(2)], axis=0)

    def own_rows(p):
        return jnp.concatenate([ref[c, p] for ref in (ekeep, epeer) for c in range(chunks)], axis=0)

    def in_turn(first, last, load, use):
        load(first, first % 2, lambda index, moves, slot: start(moves))

        @pl.loop(first, last)
        def _(p):
            at = lax.rem(p, 2)

            @pl.when(p + 1 < last)
            def _():
                load(p + 1, 1 - at, lambda index, moves, slot: start(moves))

            use(p, at)

    def with_own(slots_of):
        def load(p, at, act):
            act(0, loads(p, at), None)
            slots_of(p, at, act)
        return load

    def early(p, at):
        there = own_rows(p)
        for move in loads(p, at):
            move.wait()
        parts[0] += across(rows_of(obuf.at[at]), there)

        def add(index, moves, slot):
            for move in moves:
                move.wait()
            parts[index] += across(rows_of(abuf.at[at, slot]), there)

        early_slots(p, at, add)

    def late(p, at):
        for move in loads(p, at):
            move.wait()
        here = rows_of(obuf.at[at])

        def add(index, moves, slot):
            for move in moves:
                move.wait()
            parts[index] += across(rows_of(abuf.at[at, slot]), own_rows(p))

        late_slots(p, at, add)

        def moved(slot, plane):
            parts[3 + slot] += across(here, jnp.concatenate([lslots[slot, side, c, plane] for side, c in sides], axis=0))

        @pl.when((layer < 3) & (p >= low))
        def _():
            moved(0, p - low)

        @pl.when((layer < 2) & (p >= low))
        def _():
            moved(1, p - low)

        @pl.when((layer == 2) & (p >= more) & (p < low))
        def _():
            moved(1, p - more)

    parts[...] = jnp.zeros_like(parts)
    @on(1)
    def _():
        for side in range(2):
            arrive([r_here(1, side, q, high_cut) for q in range(2)])

    @on(3)
    def _():
        for side in range(2):
            arrive([r_here(0, side, q) for q in range(2)] + [c_move(side, extra.at[side])])

    in_turn(0, rows, with_own(early_slots), early)
    run(((pass_first, 3, 1), (pass_second, 3, 1)))

    @on(0)
    def _():
        for side, c in sides:
            arrive([l_here(slot, side, c) for slot in range(2)])

    @on(2)
    def _():
        for side, c in sides:
            l_here(1, side, c, low - more).wait_recv()

    @on(3)
    def _():
        for side in range(2):
            arrive([r_here(1, side, q) for q in range(2)])

    in_turn(0, rows, with_own(late_slots), late)

    size = parts.shape[1]
    half = size // 2
    for at in range(chunks):
        @on(at)
        def _():
            for other in range(chunks):
                if other == at:
                    turned[other] = parts[0]
                else:
                    found = [parts[i] if i in (3, 4) else parts[i].T for i in HELD[at].get(other, ())]
                    turned[other] = sum(found[1:], found[0]) if found else jnp.zeros((size, size), F32)
    for other in range(chunks):
        block = turned[other] * (1.0 / NPTS)
        block = jnp.where(line == 1, pltpu.roll(block, half, 1), block)
        sums[0, other] = block[half:]
        sums[1, other] = block[:half]
    totals = [
        remote(sums.at[0], come.at[0], sems(sum_sem, 0), "band", peer),
        remote(sums.at[2], come.at[1], sems(sum_sem, 1), "grid", me ^ 1),
        remote(sums.at[3], come.at[2], sems(sum_sem, 2), "grid", me ^ 2),
    ]
    for i, move in enumerate(totals):
        move.start()
        move.wait_recv()
        sums[2 + i] = sums[1 + i] + come[i]
    swaps = []
    for bits in range(1, chunks):
        block = sums.at[4, layer ^ bits]
        for turn in range(2):
            swaps.append((remote(
                block, last.at[bits - 1, line], sems(last_sem, bits - 1, turn), "band", band ^ (2 * bits + turn)
            ), remote(
                block, last.at[bits - 1, line ^ turn], sems(last_sem, bits - 1, turn), "band", band ^ (2 * bits + turn)
            )))
    for move, _ in swaps:
        move.start()
    gram[:, pl.ds(pl.multiple_of(layer * size, size), size)] = sums[4, layer]
    for _, move in swaps:
        move.wait_recv()
    for bits in range(1, chunks):
        whole_block = jnp.concatenate([last[bits - 1, 0], last[bits - 1, 1]], axis=0).T
        mine_block = jnp.where(line == 0, whole_block[:half], whole_block[half:])
        there = layer ^ bits
        gram[:, pl.ds(pl.multiple_of(there * size, size), size)] = sums[4, there] + mine_block

    leave(steps + picks + totals + [move for move, _ in swaps] + [oy(half) for half in range(2)])

    for c in range(chunks):
        out_move(c).wait()
        leave([ey(c, half) for half in range(2)] + forward(c)[0])
        if c >= chunks - 2:
            leave(back(c, True)[0])

    @on(0)
    def _():
        for side in range(2):
            leave([r_here(0, side, q) for q in range(2)] + [r_here(1, side, q, high_cut) for q in range(2)])

    @on(2)
    def _():
        leave([c_move(side, extra.at[side]) for side in range(2)])

    @on(1, 2)
    def _():
        for side in range(2):
            leave([r_here(slot, side, q) for slot in range(2) for q in range(2)])

    @on(1, 2, 3)
    def _():
        for side, c in sides:
            l_here(0, side, c).wait_send()

    @on(1, 2)
    def _():
        for side, c in sides:
            l_here(1, side, c).wait_send()

    @on(3)
    def _():
        for side, c in sides:
            l_here(1, side, c, low - more).wait_send()


def whole(orbitals, slab, okeep, osend, fixed):
    bands, rows, square = orbitals.shape
    groups = lax.axis_size("grid")
    chunks, count = bands // TILE, TILE // groups
    low, width = LOW * rows // 16, square // 2
    anywhere = pl.BlockSpec(memory_space=pl.ANY)
    inside = pl.BlockSpec(memory_space=pltpu.VMEM)
    dma = pltpu.SemaphoreType.DMA
    size = 2 * bands
    return pl.pallas_call(
        lambda *refs: whole_body(chunks, groups, *refs),
        in_specs=[anywhere, inside, anywhere, anywhere] + [inside] * len(fixed),
        out_specs=[anywhere] * 4 + [inside],
        out_shape=[
            jax.ShapeDtypeStruct(orbitals.shape, BF),
            jax.ShapeDtypeStruct((rows, bands, width), BF),
            jax.ShapeDtypeStruct((2, 2, low, bands, width), BF),
            jax.ShapeDtypeStruct((2, MORE, bands, width), BF),
            jax.ShapeDtypeStruct((bands, 4 * size), F32),
        ],
        scratch_shapes=[
            pltpu.VMEM((chunks, groups, count, rows, square), BF),
            pltpu.VMEM((2, groups, count, rows, square), BF),
            pltpu.VMEM((chunks, TILE, rows, square), BF),
            pltpu.VMEM((NG, square), BF),
            pltpu.VMEM((5, rows, square), BF),
            pltpu.VMEM((chunks, rows, TILE, width), BF),
            pltpu.VMEM((chunks, rows, TILE, width), BF),
            pltpu.VMEM((chunks, rows, TILE, width), BF),
            pltpu.VMEM((2, 2, chunks, low, TILE, width), BF),
            pltpu.VMEM((NG * HALF, LANES), F32),
            pltpu.VMEM((2, 2, bands, width), BF),
            pltpu.VMEM((2, 2, 2, bands, width), BF),
            pltpu.VMEM((6, size, size), F32),
            pltpu.VMEM((4, size, size), F32),
            pltpu.VMEM((5, 4, bands, size), F32),
            pltpu.VMEM((3, 4, bands, size), F32),
            pltpu.VMEM((3, 2, bands, size), F32),
            dma((2, 3)), dma((2, groups - 1)), dma((2, chunks, groups - 1)), dma((chunks,)),
            dma((2, chunks, groups - 1)), dma((chunks,)), dma((chunks,)),
            dma((2, 2)), dma((2, 2, 2, 2)), dma((2, 2)), dma((2, chunks, 2)), dma((2, 2, 2, chunks)), dma((2, 6)),
            dma((2, 3)), dma((2, 3, 2)),
        ],
        compiler_params=pltpu.CompilerParams(
            collective_id=0, has_side_effects=True, vmem_limit_bytes=60 * 1024 * 1024
        ),
        cost_estimate=pl.CostEstimate(
            flops=chunks * count * 12 * NG * NG * NG * 256, bytes_accessed=16 * orbitals.size, transcendentals=0
        ),
    )(orbitals, slab, okeep, osend, *fixed)


def flip(value, axis, bits):
    return lax.ppermute(value, axis, [(i, i ^ bits) for i in range(lax.axis_size(axis))])


def gram_body(left, right, out):
    @pl.when(pl.program_id(0) == 0)
    def _():
        out[...] = jnp.zeros_like(out)

    size = out.shape[0]
    a = left[:, 0].reshape(size, left.shape[3])
    b = right[:, 0].reshape(size, right.shape[3])
    out[...] += lax.dot_general(a, b, (((1,), (1,)), ((), ())), preferred_element_type=F32)


def gram_product(left, right):
    shares, planes, bands, points = left.shape
    size = shares * bands
    if bands % 16 or points % 128:
        return jnp.einsum("gxbk,hxck->gbhc", left, right, preferred_element_type=F32).reshape(size, size)
    block = pl.BlockSpec((shares, 1, bands, points), lambda i: (0, i, 0, 0))
    return pl.pallas_call(
        gram_body,
        grid=(planes,),
        in_specs=[block, block],
        out_specs=pl.BlockSpec((size, size), lambda i: (0, 0)),
        out_shape=jax.ShapeDtypeStruct((size, size), F32),
        compiler_params=pltpu.CompilerParams(vmem_limit_bytes=32 * 1024 * 1024),
        cost_estimate=pl.CostEstimate(
            flops=2 * size * size * planes * points, bytes_accessed=4 * left.size, transcendentals=0
        ),
    )(left, right)


def to_shares(array):
    shares = lax.axis_size("band")
    bands, planes, square = array.shape
    cut = array.reshape(bands, planes, shares, square // shares).transpose(2, 1, 0, 3)
    return lax.all_to_all(cut, "band", split_axis=0, concat_axis=0)


def spread(slab):
    bit = 1
    while bit < lax.axis_size("band"):
        slab = slab + flip(slab, "band", bit)
        bit *= 2
    groups = lax.axis_size("grid")
    return jnp.concatenate([slab] + [flip(slab, "grid", d) for d in range(1, groups)], axis=0)


def per_device(orbitals, picks):
    bands, planes, square = orbitals.shape
    groups, shares = lax.axis_size("grid"), lax.axis_size("band")
    me = lax.axis_index("grid")
    fixed = factors(groups)
    target = picks[0]
    mine = lax.dynamic_index_in_dim(orbitals, target % bands, 0, keepdims=False)
    slab = jnp.where(lax.axis_index("band") == target // bands, mine, 0).astype(BF)

    if shares == 8 and groups == 4 and bands == 4 * TILE and planes == 16:
        vectors, _, _, _, gram = whole(orbitals, slab, *order_orbitals(orbitals), fixed)
        return (vectors, gram)

    partner = spread(slab)
    count = bands // groups
    pieces = []
    for d in range(groups):
        part = lax.dynamic_slice_in_dim(orbitals, (me ^ d) * count, count, 0)
        pieces.append(flip(part, "grid", d) if d else part)
    solved = solve(pieces, partner, fixed)
    back = [flip(p, "grid", d) if d else p for d, p in enumerate(solved)]
    stacked = jnp.take(jnp.stack(back), me ^ jnp.arange(groups), axis=0)
    vectors = stacked.reshape(bands, planes, square)
    product = gram_product(to_shares(orbitals), to_shares(vectors))
    rows = lax.psum_scatter(product * (1.0 / NPTS), "band", scatter_dimension=0, tiled=True)
    return (vectors, lax.psum(rows, "grid"))


def solution(mesh):
    return jax.shard_map(
        per_device,
        mesh=mesh,
        in_specs=(P("band", "grid", None), P()),
        out_specs=(P("band", "grid", None), P("band", None)),
        check_vma=False,
    )
```

```python
import math
import jax
import jax.numpy as jnp
import ml_dtypes
import numpy as np
from jax import lax
from jax.experimental import pallas as pl
from jax.experimental.pallas import tpu as pltpu
from jax.sharding import PartitionSpec as P

NG = 64
NPTS = NG ** 3
KERNEL_SCALE = 128.0
LANES = 128
BF = ml_dtypes.bfloat16
F32 = jnp.float32
HALF = NG // 2
XW = 512
PLANES = 32
TILE = 16
SWAP = 256
LOW = 9
MORE = 3
HELD = ({2: (3,), 3: (4,)}, {0: (1, 2), 2: (3,), 3: (4,)}, {1: (1,), 0: (2,), 3: (3, 4)}, {1: (1,), 0: (2,), 2: (5,)})


def cas_matrix(length):
    products = np.arange(length)[:, None] * np.arange(length)[None, :] % length
    angles = products * (2.0 * math.pi / length)
    return (np.cos(angles) + np.sin(angles)).astype(np.float32)


def halves(value):
    high = value.astype(BF)
    return high, (value - high.astype(F32)).astype(BF)


def kernel_table():
    frequency = np.arange(NG)
    folded = np.minimum(frequency, NG - frequency)
    square = folded * folded
    summed = square[:, None, None] + square[None, :, None] + square[None, None, :]
    table = np.where(summed > 0, KERNEL_SCALE / NPTS / np.maximum(summed, 1), 0.0).astype(np.float32)
    return table.reshape(NG // 4, 4, NG, NG).transpose(0, 2, 1, 3).reshape(NG // 4, NG, 4 * NG)


def row_factor(matrix):
    high, low = halves(matrix)
    return np.concatenate([high, high, low], axis=1)


def lane_factor(matrix):
    high, low = halves(np.kron(np.eye(2, dtype=np.float32), matrix))
    upper = np.concatenate([high, low], axis=1)
    lower = np.concatenate([high, np.zeros_like(low)], axis=1)
    return np.concatenate([upper, lower], axis=0)


def dot(a, b):
    return jnp.dot(a, b, preferred_element_type=F32)


def solve_one(ins, partner, table, x_there, x_back, y_there, y_back, z_both, outs, work):
    rows = NG // len(ins)
    me = lax.axis_index("grid")
    x_there, x_back = x_there.at[me], x_back.at[me]

    def along_rows(factor, value):
        high, low = halves(value)
        return dot(factor[...], jnp.concatenate([high, low, high], axis=0))

    def along_lanes(value):
        high, low = halves(value)
        both = dot(jnp.concatenate([high, low], axis=1), z_both[...])
        return both[:, :LANES] + both[:, LANES:]

    @pl.loop(0, NG * NG // XW, unroll=4)
    def _(i):
        at = pl.ds(pl.multiple_of(i * XW, XW), XW)
        field = jnp.concatenate([ref[:, at].astype(F32) for ref in ins], axis=0)
        field = along_rows(x_there, field * partner[:, at].astype(F32))
        for tile in range(XW // LANES):
            work[pl.ds(i * (XW // LANES) + tile, NG, stride=HALF), :] = field[:, tile * LANES:(tile + 1) * LANES]

    @pl.loop(0, NG // PLANES, unroll=2)
    def _(i):
        left = lax.broadcasted_iota(jnp.int32, (HALF, LANES), 1) < NG
        base = i * PLANES * HALF
        parts = []
        for pair in range(PLANES // 2):
            a = work[pl.ds(base + pair * NG, HALF), :]
            b = work[pl.ds(base + pair * NG + HALF, HALF), :]
            parts.append(jnp.where(left, a, pltpu.roll(b, NG, 1)))
            parts.append(jnp.where(left, pltpu.roll(a, NG, 1), b))
        field = along_lanes(jnp.concatenate(parts, axis=0))
        done = []
        for quad in range(PLANES // 4):
            wide = jnp.concatenate(
                [field[quad * 128:quad * 128 + 64], field[quad * 128 + 64:quad * 128 + 128]], axis=1
            )
            wide = along_rows(y_there, wide) * table[i * (PLANES // 4) + quad]
            wide = along_rows(y_back, wide)
            done.append(wide[:, :LANES])
            done.append(wide[:, LANES:])
        field = along_lanes(jnp.concatenate(done, axis=0))
        for pair in range(PLANES // 2):
            u = field[pair * NG:pair * NG + HALF]
            v = field[pair * NG + HALF:pair * NG + NG]
            work[pl.ds(base + pair * NG, HALF), :] = jnp.where(left, u, pltpu.roll(v, NG, 1))
            work[pl.ds(base + pair * NG + HALF, HALF), :] = jnp.where(left, pltpu.roll(u, NG, 1), v)

    @pl.loop(0, NG * NG // XW, unroll=4)
    def _(i):
        at = pl.ds(pl.multiple_of(i * XW, XW), XW)
        field = jnp.concatenate(
            [work[pl.ds(i * (XW // LANES) + tile, NG, stride=HALF), :] for tile in range(XW // LANES)], axis=1
        )
        field = (-along_rows(x_back, field) * partner[:, at].astype(F32)).astype(BF)
        for index, ref in enumerate(outs):
            ref[:, at] = field[index * rows:(index + 1) * rows]


def solve_body(groups, *refs):
    ins, outs = refs[:groups], refs[groups + 7:2 * groups + 7]
    solve_one([ref.at[0] for ref in ins], *refs[groups:groups + 7], [ref.at[0] for ref in outs], refs[-1])


def factors(groups):
    matrix = cas_matrix(NG)
    there, back = [], []
    for me in range(groups):
        order = [slab * (NG // groups) + plane for slab in (me ^ d for d in range(groups)) for plane in range(NG // groups)]
        there.append(row_factor(matrix[:, order]))
        back.append(row_factor(matrix[:, order].T))
    by_line = matrix.reshape(NG, HALF, 2).transpose(0, 2, 1).reshape(NG, NG)
    return [jnp.asarray(value) for value in (
        kernel_table(), np.stack(there), np.stack(back),
        row_factor(by_line), row_factor(by_line.T), lane_factor(matrix),
    )]


def solve(pieces, partner, fixed):
    groups = len(pieces)
    count, rows, square = pieces[0].shape
    block = pl.BlockSpec((1, rows, square), lambda i: (i, 0, 0))
    whole = lambda array: pl.BlockSpec(array.shape, lambda i: (0,) * array.ndim)
    fixed = (partner,) + tuple(fixed)
    return pl.pallas_call(
        lambda *refs: solve_body(groups, *refs),
        grid=(count,),
        in_specs=[block] * groups + [whole(a) for a in fixed],
        out_specs=[block] * groups,
        out_shape=[jax.ShapeDtypeStruct(p.shape, BF) for p in pieces],
        scratch_shapes=[pltpu.VMEM((NG * HALF, LANES), F32)],
        compiler_params=pltpu.CompilerParams(vmem_limit_bytes=32 * 1024 * 1024),
        cost_estimate=pl.CostEstimate(
            flops=count * 12 * NG * NG * NG * 256, bytes_accessed=4 * count * NPTS, transcendentals=0
        ),
    )(*pieces, *fixed)
def swap_into(held, keep, send):
    width = held.shape[2] // 2
    mine = lax.axis_index("band") % 2

    @pl.loop(0, width // SWAP)
    def _(i):
        put = pl.ds(pl.multiple_of(i * SWAP, SWAP), SWAP)
        for at, out in ((mine, keep), (1 - mine, send)):
            lanes = pl.ds(pl.multiple_of(at * width + i * SWAP, SWAP), SWAP)
            out[:, :, put] = jnp.swapaxes(held[:, :, lanes], 0, 1)


def order_orbitals(orbitals):
    bands, rows, square = orbitals.shape
    part = jax.ShapeDtypeStruct((rows, bands, square // 2), BF)
    spec = pl.BlockSpec((rows, TILE, square // 2), lambda i: (0, i, 0))
    return pl.pallas_call(
        swap_into,
        grid=(bands // TILE,),
        in_specs=[pl.BlockSpec((TILE, rows, square), lambda i: (i, 0, 0))],
        out_specs=[spec] * 2,
        out_shape=[part] * 2,
        compiler_params=pltpu.CompilerParams(vmem_limit_bytes=60 * 1024 * 1024),
        cost_estimate=pl.CostEstimate(flops=0, bytes_accessed=4 * orbitals.size, transcendentals=0),
    )(orbitals)


def whole_body(chunks, groups, *refs):
    (orb, slab, okeep, osend, table, x_there, x_back, y_there, y_back, z_both,
     vectors, opeer, slots, extra, gram,
     cubes, solved, fresh, partner, hyper, ekeep, epeer, esend, lslots, work, obuf, abuf,
     parts, turned, sums, come, last,
     hyper_sem, pick_sem, fwd_sem, own_sem, back_sem, stay_sem, out_sem,
     oy_sem, r_sem, c_sem, ey_sem, l_sem, load_sem, sum_sem, last_sem) = refs
    count, rows = cubes.shape[2:4]
    low = lslots.shape[3]
    high = rows - low
    more = extra.shape[1]
    band, me = lax.axis_index("band"), lax.axis_index("grid")
    layer, line = band // 2, band % 2
    peer = band ^ 1
    up, down = lax.rem(band + 2, 8), lax.rem(band + 6, 8)

    def remote(source, target, sems, axis, index):
        return pltpu.make_async_remote_copy(
            src_ref=source, dst_ref=target, send_sem=sems[0], recv_sem=sems[1],
            device_id={axis: index}, device_id_type=pl.DeviceIdType.MESH,
        )

    def sems(array, *at):
        return array.at[(0,) + at], array.at[(1,) + at]

    def start(moves):
        for move in moves:
            move.start()

    def arrive(moves):
        for move in moves:
            move.wait_recv()

    def leave(moves):
        for move in moves:
            move.wait_send()

    def on(*layers):
        hit = layer == layers[0]
        for other in layers[1:]:
            hit = hit | (layer == other)
        return pl.when(hit)

    barrier = pltpu.get_barrier_semaphore()
    for bits in range(1, 8):
        pl.semaphore_signal(barrier, inc=1, device_id={"band": band ^ bits}, device_id_type=pl.DeviceIdType.MESH)
    for d in range(1, groups):
        pl.semaphore_signal(barrier, inc=1, device_id={"grid": me ^ d}, device_id_type=pl.DeviceIdType.MESH)
    pl.semaphore_wait(barrier, 6 + groups)

    def forward(c):
        def at(d):
            return orb.at[pl.ds(c * TILE + (me ^ d) * count, count)]
        moves = [remote(at(d), cubes.at[c, d], sems(fwd_sem, c, d - 1), "grid", me ^ d) for d in range(1, groups)]
        return moves, pltpu.make_async_copy(at(0), cubes.at[c, 0], own_sem.at[c])

    def start_forward(c):
        moves, stay = forward(c)
        start(moves)
        stay.start()

    def wait_forward(c):
        moves, stay = forward(c)
        arrive(moves)
        stay.wait()

    def back(c, mine):
        def at(d):
            return fresh.at[c, pl.ds((me if mine else me ^ d) * count, count)]
        moves = [remote(solved.at[c % 2, d], at(d), sems(back_sem, c, d - 1), "grid", me ^ d) for d in range(1, groups)]
        own = fresh.at[c, pl.ds(me * count, count)]
        return moves, pltpu.make_async_copy(solved.at[c % 2, 0], own, stay_sem.at[c])

    def start_back(c):
        moves, stay = back(c, True)
        start(moves)
        stay.start()

    def free_solved(c):
        leave(back(c, True)[0])

    low_cut = ((0, (low + 1) // 2), ((low + 1) // 2, low // 2))
    high_cut = ((0, (high + 1) // 2), ((high + 1) // 2, high // 2))

    def r_move(slot, side, q, source, first=0, cut=low_cut):
        at, size = cut[q]
        return remote(
            source.at[pl.ds(first + at, size)], slots.at[slot, side, pl.ds(at, size)],
            sems(r_sem, slot, side, q), "band", up,
        )

    def r_pass(slot, side, q, onto):
        return r_move(onto, side, q, slots.at[slot, side])

    def r_here(slot, side, q, cut=low_cut):
        return r_move(slot, side, q, slots.at[slot, side], 0, cut)

    def c_move(side, source):
        return remote(source.at[pl.ds(0, more)], extra.at[side], sems(c_sem, side), "band", up)

    def l_move(slot, side, c, source, first, size):
        return remote(
            source.at[pl.ds(first, size)], lslots.at[slot, side, c, pl.ds(0, size)],
            sems(l_sem, slot, side, c), "band", down,
        )

    def l_here(slot, side, c, size=high):
        return l_move(slot, side, c, lslots.at[slot, side, c], 0, size)

    def oy(half):
        at = pl.ds(low, high) if half else pl.ds(0, low)
        return remote(osend.at[at], opeer.at[at], sems(oy_sem, half), "band", peer)

    def ey(c, half):
        at = pl.ds(low, high) if half else pl.ds(0, low)
        return remote(esend.at[c, at], epeer.at[c, at], sems(ey_sem, c, half), "band", peer)

    steps = [remote(slab, hyper.at[0], sems(hyper_sem, 0), "band", band ^ 1)]
    steps.append(remote(hyper.at[3], hyper.at[1], sems(hyper_sem, 1), "band", band ^ 2))
    steps.append(remote(hyper.at[4], hyper.at[2], sems(hyper_sem, 2), "band", band ^ 4))
    mine = pl.ds(0, rows)
    picks = [
        remote(partner.at[mine], partner.at[pl.ds(d * rows, rows)], sems(pick_sem, d - 1), "grid", me ^ d)
        for d in range(1, groups)
    ]
    steps[0].start()
    start_forward(0)
    steps[0].wait_recv()
    hyper[3] = slab[...] + hyper[0]
    steps[1].start()
    oy(0).start()
    steps[1].wait_recv()
    hyper[4] = hyper[3] + hyper[1]
    steps[2].start()

    @on(0, 1)
    def _():
        start([r_move(0, 0, q, okeep) for q in range(2)])

    @on(2)
    def _():
        c_move(0, okeep).start()

    steps[2].wait_recv()
    partner[mine] = hyper[4] + hyper[2]
    start(picks)
    oy(1).start()

    def own_orbitals(q):
        @on(1)
        def _():
            r_here(0, 0, q).wait_recv()
            r_pass(0, 0, q, 1).start()

        @on(2)
        def _():
            r_here(0, 0, q).wait_recv()
            r_pass(0, 0, q, 0).start()

        @on(0)
        def _():
            r_move(1, 0, q, okeep, low, high_cut).start()

    def own_orbitals_on(q):
        @on(2)
        def _():
            r_here(1, 0, q).wait_recv()
            r_pass(1, 0, q, 1).start()

        if q == 0:
            oy(0).wait_recv()

            @on(0, 1)
            def _():
                start([r_move(0, 1, part, opeer) for part in range(2)])

            @on(2)
            def _():
                c_move(1, opeer).start()

    def peer_orbitals(q):
        if q == 0:
            oy(1).wait_recv()

        @on(1)
        def _():
            r_here(0, 1, q).wait_recv()
            r_pass(0, 1, q, 1).start()

        @on(2)
        def _():
            r_here(0, 1, q).wait_recv()
            r_pass(0, 1, q, 0).start()

        @on(0)
        def _():
            r_move(1, 1, q, opeer, low, high_cut).start()

    def peer_orbitals_on(q):
        @on(2)
        def _():
            r_here(1, 1, q).wait_recv()
            r_pass(1, 1, q, 1).start()

    def out_move(c):
        return pltpu.make_async_copy(fresh.at[c], vectors.at[pl.ds(c * TILE, TILE)], out_sem.at[c])

    def collect(c):
        moves, stay = back(c, False)
        arrive(moves)
        stay.wait()
        out_move(c).start()
        swap_into(fresh.at[c], ekeep.at[c], esend.at[c])
        ey(c, 1).start()
        send_vectors(c, 0)
        ey(c, 0).start()

    def send_vectors(c, side):
        source = (epeer if side else ekeep).at[c]
        if side:
            ey(c, 1).wait_recv()

        @on(2, 3)
        def _():
            l_move(0, side, c, source, low, high).start()

        if side:
            ey(c, 0).wait_recv()

        @on(3)
        def _():
            l_move(1, side, c, source, more, low - more).start()

    def pass_first(c, side):
        @on(2)
        def _():
            l_here(0, side, c).wait_recv()
            l_move(1, side, c, lslots.at[0, side, c], 0, high).start()

        @on(1)
        def _():
            l_here(0, side, c).wait_recv()
            l_move(0, side, c, lslots.at[0, side, c], 0, high).start()

    def pass_second(c, side):
        @on(1)
        def _():
            l_here(1, side, c).wait_recv()
            l_move(1, side, c, lslots.at[1, side, c], 0, high).start()

    arrive(picks)
    start_forward(1)
    before = {
        0: [(wait_forward, 0)],
        4: [(wait_forward, 1)],
        8: [(pass_first, 0, 0), (own_orbitals_on, 0), (wait_forward, 2), (free_solved, 0)],
        12: [(pass_second, 0, 1), (pass_first, 1, 0), (wait_forward, 3), (free_solved, 1)],
    }
    after = {
        0: [(own_orbitals, 0)],
        3: [(start_back, 0)],
        4: [(own_orbitals, 1)],
        5: [(start_forward, 2)],
        7: [(start_back, 1), (collect, 0)],
        8: [(pass_second, 0, 0)],
        9: [(start_forward, 3), (send_vectors, 0, 1)],
        11: [(start_back, 2), (pass_first, 0, 1), (own_orbitals_on, 1), (collect, 1)],
        12: [(send_vectors, 1, 1), (pass_second, 1, 0)],
        13: [(peer_orbitals, 0)],
        15: [(start_back, 3), (pass_first, 1, 1), (collect, 2)],
    }

    def run(events):
        for event in events:
            event[0](*event[1:])

    def at_slot(t, table):
        for slot, events in table.items():
            @pl.when(t == slot)
            def _():
                run(events)

    @pl.loop(0, chunks * count)
    def _(t):
        at_slot(t, before)
        c, j = t // count, lax.rem(t, count)
        solve_one(
            [cubes.at[c, d, j] for d in range(groups)], partner, table, x_there, x_back,
            y_there, y_back, z_both, [solved.at[lax.rem(c, 2), d, j] for d in range(groups)], work,
        )
        at_slot(t, after)

    run((
        (pass_second, 1, 1), (peer_orbitals, 1), (pass_first, 2, 0), (send_vectors, 2, 1), (pass_second, 2, 0),
        (peer_orbitals_on, 0), (pass_first, 2, 1), (collect, 3), (pass_second, 2, 1),
        (peer_orbitals_on, 1), (pass_first, 3, 0), (send_vectors, 3, 1), (pass_second, 3, 0),
    ))

    sides = [(side, c) for side in range(2) for c in range(chunks)]

    def loads(p, at):
        return [
            pltpu.make_async_copy(source.at[p], obuf.at[at, side], load_sem.at[at, side])
            for side, source in enumerate((okeep, opeer))
        ]

    def slot_loads(slot, p, at):
        return [
            pltpu.make_async_copy(slots.at[slot, side, p], abuf.at[at, slot, side], load_sem.at[at, 2 + slot * 2 + side])
            for side in range(2)
        ]

    def extra_loads(p, at):
        return [
            pltpu.make_async_copy(extra.at[side, p], abuf.at[at, 1, side], load_sem.at[at, 4 + side])
            for side in range(2)
        ]

    def early_slots(p, at, act):
        @pl.when((layer > 0) & (p < low))
        def _():
            act(1, slot_loads(0, p, at), 0)

        @pl.when((layer == 2) & (p < low))
        def _():
            act(2, slot_loads(1, p, at), 1)

        @pl.when((layer == 1) & (p >= low))
        def _():
            act(2, slot_loads(1, p - low, at), 1)

        @pl.when((layer == 3) & (p < more))
        def _():
            act(5, extra_loads(p, at), 1)

    def late_slots(p, at, act):
        @pl.when((layer == 3) & (p < low))
        def _():
            act(2, slot_loads(1, p, at), 1)

    def across(a, b):
        return lax.dot_general(a, b, (((1,), (1,)), ((), ())), preferred_element_type=F32)

    def rows_of(buffer):
        return jnp.concatenate([buffer[side] for side in range(2)], axis=0)

    def own_rows(p):
        return jnp.concatenate([ref[c, p] for ref in (ekeep, epeer) for c in range(chunks)], axis=0)

    def in_turn(first, last, load, use):
        load(first, first % 2, lambda index, moves, slot: start(moves))

        @pl.loop(first, last)
        def _(p):
            at = lax.rem(p, 2)

            @pl.when(p + 1 < last)
            def _():
                load(p + 1, 1 - at, lambda index, moves, slot: start(moves))

            use(p, at)

    def with_own(slots_of):
        def load(p, at, act):
            act(0, loads(p, at), None)
            slots_of(p, at, act)
        return load

    def early(p, at):
        there = own_rows(p)
        for move in loads(p, at):
            move.wait()
        parts[0] += across(rows_of(obuf.at[at]), there)

        def add(index, moves, slot):
            for move in moves:
                move.wait()
            parts[index] += across(rows_of(abuf.at[at, slot]), there)

        early_slots(p, at, add)

    def late(p, at):
        for move in loads(p, at):
            move.wait()
        here = rows_of(obuf.at[at])

        def add(index, moves, slot):
            for move in moves:
                move.wait()
            parts[index] += across(rows_of(abuf.at[at, slot]), own_rows(p))

        late_slots(p, at, add)

        def moved(slot, plane):
            parts[3 + slot] += across(here, jnp.concatenate([lslots[slot, side, c, plane] for side, c in sides], axis=0))

        @pl.when((layer < 3) & (p >= low))
        def _():
            moved(0, p - low)

        @pl.when((layer < 2) & (p >= low))
        def _():
            moved(1, p - low)

        @pl.when((layer == 2) & (p >= more) & (p < low))
        def _():
            moved(1, p - more)

    parts[...] = jnp.zeros_like(parts)
    @on(1)
    def _():
        for side in range(2):
            arrive([r_here(1, side, q, high_cut) for q in range(2)])

    @on(3)
    def _():
        for side in range(2):
            arrive([r_here(0, side, q) for q in range(2)] + [c_move(side, extra.at[side])])

    in_turn(0, rows, with_own(early_slots), early)
    run(((pass_first, 3, 1), (pass_second, 3, 1)))

    @on(0)
    def _():
        for side, c in sides:
            arrive([l_here(slot, side, c) for slot in range(2)])

    @on(2)
    def _():
        for side, c in sides:
            l_here(1, side, c, low - more).wait_recv()

    @on(3)
    def _():
        for side in range(2):
            arrive([r_here(1, side, q) for q in range(2)])

    in_turn(0, rows, with_own(late_slots), late)

    size = parts.shape[1]
    half = size // 2
    for at in range(chunks):
        @on(at)
        def _():
            for other in range(chunks):
                if other == at:
                    turned[other] = parts[0]
                else:
                    found = [parts[i] if i in (3, 4) else parts[i].T for i in HELD[at].get(other, ())]
                    turned[other] = sum(found[1:], found[0]) if found else jnp.zeros((size, size), F32)
    for other in range(chunks):
        block = turned[other] * (1.0 / NPTS)
        block = jnp.where(line == 1, pltpu.roll(block, half, 1), block)
        sums[0, other] = block[half:]
        sums[1, other] = block[:half]
    totals = [
        remote(sums.at[0], come.at[0], sems(sum_sem, 0), "band", peer),
        remote(sums.at[2], come.at[1], sems(sum_sem, 1), "grid", me ^ 1),
        remote(sums.at[3], come.at[2], sems(sum_sem, 2), "grid", me ^ 2),
    ]
    for i, move in enumerate(totals):
        move.start()
        move.wait_recv()
        sums[2 + i] = sums[1 + i] + come[i]
    swaps = []
    for bits in range(1, chunks):
        block = sums.at[4, layer ^ bits]
        for turn in range(2):
            swaps.append((remote(
                block, last.at[bits - 1, line], sems(last_sem, bits - 1, turn), "band", band ^ (2 * bits + turn)
            ), remote(
                block, last.at[bits - 1, line ^ turn], sems(last_sem, bits - 1, turn), "band", band ^ (2 * bits + turn)
            )))
    for move, _ in swaps:
        move.start()
    gram[:, pl.ds(pl.multiple_of(layer * size, size), size)] = sums[4, layer]
    for _, move in swaps:
        move.wait_recv()
    for bits in range(1, chunks):
        whole_block = jnp.concatenate([last[bits - 1, 0], last[bits - 1, 1]], axis=0).T
        mine_block = jnp.where(line == 0, whole_block[:half], whole_block[half:])
        there = layer ^ bits
        gram[:, pl.ds(pl.multiple_of(there * size, size), size)] = sums[4, there] + mine_block

    leave(steps + picks + totals + [move for move, _ in swaps] + [oy(half) for half in range(2)])

    for c in range(chunks):
        out_move(c).wait()
        leave([ey(c, half) for half in range(2)] + forward(c)[0])
        if c >= chunks - 2:
            leave(back(c, True)[0])

    @on(0)
    def _():
        for side in range(2):
            leave([r_here(0, side, q) for q in range(2)] + [r_here(1, side, q, high_cut) for q in range(2)])

    @on(2)
    def _():
        leave([c_move(side, extra.at[side]) for side in range(2)])

    @on(1, 2)
    def _():
        for side in range(2):
            leave([r_here(slot, side, q) for slot in range(2) for q in range(2)])

    @on(1, 2, 3)
    def _():
        for side, c in sides:
            l_here(0, side, c).wait_send()

    @on(1, 2)
    def _():
        for side, c in sides:
            l_here(1, side, c).wait_send()

    @on(3)
    def _():
        for side, c in sides:
            l_here(1, side, c, low - more).wait_send()


def whole(orbitals, slab, okeep, osend, fixed):
    bands, rows, square = orbitals.shape
    groups = lax.axis_size("grid")
    chunks, count = bands // TILE, TILE // groups
    low, width = LOW * rows // 16, square // 2
    anywhere = pl.BlockSpec(memory_space=pl.ANY)
    inside = pl.BlockSpec(memory_space=pltpu.VMEM)
    dma = pltpu.SemaphoreType.DMA
    size = 2 * bands
    return pl.pallas_call(
        lambda *refs: whole_body(chunks, groups, *refs),
        in_specs=[anywhere, inside, anywhere, anywhere] + [inside] * len(fixed),
        out_specs=[anywhere] * 4 + [inside],
        out_shape=[
            jax.ShapeDtypeStruct(orbitals.shape, BF),
            jax.ShapeDtypeStruct((rows, bands, width), BF),
            jax.ShapeDtypeStruct((2, 2, low, bands, width), BF),
            jax.ShapeDtypeStruct((2, MORE, bands, width), BF),
            jax.ShapeDtypeStruct((bands, 4 * size), F32),
        ],
        scratch_shapes=[
            pltpu.VMEM((chunks, groups, count, rows, square), BF),
            pltpu.VMEM((2, groups, count, rows, square), BF),
            pltpu.VMEM((chunks, TILE, rows, square), BF),
            pltpu.VMEM((NG, square), BF),
            pltpu.VMEM((5, rows, square), BF),
            pltpu.VMEM((chunks, rows, TILE, width), BF),
            pltpu.VMEM((chunks, rows, TILE, width), BF),
            pltpu.VMEM((chunks, rows, TILE, width), BF),
            pltpu.VMEM((2, 2, chunks, low, TILE, width), BF),
            pltpu.VMEM((NG * HALF, LANES), F32),
            pltpu.VMEM((2, 2, bands, width), BF),
            pltpu.VMEM((2, 2, 2, bands, width), BF),
            pltpu.VMEM((6, size, size), F32),
            pltpu.VMEM((4, size, size), F32),
            pltpu.VMEM((5, 4, bands, size), F32),
            pltpu.VMEM((3, 4, bands, size), F32),
            pltpu.VMEM((3, 2, bands, size), F32),
            dma((2, 3)), dma((2, groups - 1)), dma((2, chunks, groups - 1)), dma((chunks,)),
            dma((2, chunks, groups - 1)), dma((chunks,)), dma((chunks,)),
            dma((2, 2)), dma((2, 2, 2, 2)), dma((2, 2)), dma((2, chunks, 2)), dma((2, 2, 2, chunks)), dma((2, 6)),
            dma((2, 3)), dma((2, 3, 2)),
        ],
        compiler_params=pltpu.CompilerParams(
            collective_id=0, has_side_effects=True, vmem_limit_bytes=60 * 1024 * 1024
        ),
        cost_estimate=pl.CostEstimate(
            flops=chunks * count * 12 * NG * NG * NG * 256, bytes_accessed=16 * orbitals.size, transcendentals=0
        ),
    )(orbitals, slab, okeep, osend, *fixed)


def flip(value, axis, bits):
    return lax.ppermute(value, axis, [(i, i ^ bits) for i in range(lax.axis_size(axis))])


def gram_body(left, right, out):
    @pl.when(pl.program_id(0) == 0)
    def _():
        out[...] = jnp.zeros_like(out)

    size = out.shape[0]
    a = left[:, 0].reshape(size, left.shape[3])
    b = right[:, 0].reshape(size, right.shape[3])
    out[...] += lax.dot_general(a, b, (((1,), (1,)), ((), ())), preferred_element_type=F32)


def gram_product(left, right):
    shares, planes, bands, points = left.shape
    size = shares * bands
    if bands % 16 or points % 128:
        return jnp.einsum("gxbk,hxck->gbhc", left, right, preferred_element_type=F32).reshape(size, size)
    block = pl.BlockSpec((shares, 1, bands, points), lambda i: (0, i, 0, 0))
    return pl.pallas_call(
        gram_body,
        grid=(planes,),
        in_specs=[block, block],
        out_specs=pl.BlockSpec((size, size), lambda i: (0, 0)),
        out_shape=jax.ShapeDtypeStruct((size, size), F32),
        compiler_params=pltpu.CompilerParams(vmem_limit_bytes=32 * 1024 * 1024),
        cost_estimate=pl.CostEstimate(
            flops=2 * size * size * planes * points, bytes_accessed=4 * left.size, transcendentals=0
        ),
    )(left, right)


def to_shares(array):
    shares = lax.axis_size("band")
    bands, planes, square = array.shape
    cut = array.reshape(bands, planes, shares, square // shares).transpose(2, 1, 0, 3)
    return lax.all_to_all(cut, "band", split_axis=0, concat_axis=0)


def spread(slab):
    bit = 1
    while bit < lax.axis_size("band"):
        slab = slab + flip(slab, "band", bit)
        bit *= 2
    groups = lax.axis_size("grid")
    return jnp.concatenate([slab] + [flip(slab, "grid", d) for d in range(1, groups)], axis=0)


def per_device(orbitals, picks):
    bands, planes, square = orbitals.shape
    groups, shares = lax.axis_size("grid"), lax.axis_size("band")
    me = lax.axis_index("grid")
    fixed = factors(groups)
    target = picks[0]
    mine = lax.dynamic_index_in_dim(orbitals, target % bands, 0, keepdims=False)
    slab = jnp.where(lax.axis_index("band") == target // bands, mine, 0).astype(BF)

    if shares == 8 and groups == 4 and bands == 4 * TILE and planes == 16:
        vectors, _, _, _, gram = whole(orbitals, slab, *order_orbitals(orbitals), fixed)
        return (vectors, gram)

    partner = spread(slab)
    count = bands // groups
    pieces = []
    for d in range(groups):
        part = lax.dynamic_slice_in_dim(orbitals, (me ^ d) * count, count, 0)
        pieces.append(flip(part, "grid", d) if d else part)
    solved = solve(pieces, partner, fixed)
    back = [flip(p, "grid", d) if d else p for d, p in enumerate(solved)]
    stacked = jnp.take(jnp.stack(back), me ^ jnp.arange(groups), axis=0)
    vectors = stacked.reshape(bands, planes, square)
    product = gram_product(to_shares(orbitals), to_shares(vectors))
    rows = lax.psum_scatter(product * (1.0 / NPTS), "band", scatter_dimension=0, tiled=True)
    return (vectors, lax.psum(rows, "grid"))


def solution(mesh):
    return jax.shard_map(
        per_device,
        mesh=mesh,
        in_specs=(P("band", "grid", None), P()),
        out_specs=(P("band", "grid", None), P("band", None)),
        check_vma=False,
    )
```
